512 devices in a mesh: row: 32 (over z, core), col: 16 (over y, x).
Axes of the slice: x: 4, y: 4, z: 16, core: 2. Of those that a mesh axis runs over, the one named last changes fastest.
Arguments:
- a_blocks: bfloat16 [32, 16, 16, 320, 320], P('row', 'col'), may hold values from -0.3125 to 0.3125
- slot_row: int32 [32, 16, 16], P('row', 'col'), may hold values from 0 to 3
- slot_col: int32 [32, 16, 16], P('row', 'col'), may hold values from 0 to 7
- slot_count: int32 [32, 16], P('row', 'col'), may hold values from 1 to 16, as said below
- p_blocks: bfloat16 [128, 320, 64], P('row'), may hold values from -1.5 to 1.5
- aggregate: int32 [128], P('row'), may hold values from 0 to 31
- relayout: int32 [32], replicated, may hold values from 0 to 31, as said below
Outputs:
- coarse_relaid: float32 [32, 64, 2048], P('row')
The draws below stay inside these ranges and needn't reach their ends.
Inputs may be any that keep to these rules, and one draw needn't show every extreme that they name: `slot_count`: each list holds 1 to 16 live blocks, and some list holds 16 in every draw. relayout is a permutation of the 32 coarse block rows.
All inputs are finite; a program needn't handle non-finite values.
Results may differ from the reference program's by a relative error of at most 0.0003.
Values may be sent and summed in bfloat16 or wider, within the bound.
A program may use at most 64 MiB of HBM per device.

```python
import jax
import jax.numpy as jnp
from jax import lax

BLK = 320
BC = 64
FB_DEV = 4
SLOTS = 16
NFB = 128
CB_DEV = 8
NC = 32
N_ROW = 32
N_COL = 16


def draw_slot_count(key, part):
    key = jax.random.fold_in(key, 11)
    first_key, second_key, third_key = jax.random.split(key, 3)
    first = jax.random.randint(first_key, (N_ROW, N_COL), 0, SLOTS)
    second = jax.random.randint(second_key, (N_ROW, N_COL), 0, SLOTS)
    counts = 1 + first * second // SLOTS
    chosen = jax.random.randint(third_key, (), 0, N_ROW * N_COL)
    places = jnp.arange(N_ROW * N_COL, dtype=jnp.int32).reshape(N_ROW, N_COL)
    return jnp.where(places == chosen, SLOTS, counts).astype(jnp.int32)


def place_value(order, position, value):
    where_now = jnp.argmax((order == value).astype(jnp.int32)).astype(jnp.int32)
    previous = order[position]
    order = order.at[where_now].set(previous)
    return order.at[position].set(value)


def draw_relayout(key, part):
    key = jax.random.fold_in(key, 23)
    keys = jax.random.split(key, 8)
    per_dev = NC // N_ROW
    order = jax.random.permutation(keys[0], NC).astype(jnp.int32)
    start = jax.random.randint(keys[1], (), 0, N_ROW)
    sources = (start - 1, start + 1 + N_ROW // 2, start + 3)
    for step in range(3):
        target_dev = (start + step) % N_ROW
        source_dev = sources[step] % N_ROW
        position = target_dev * per_dev + jax.random.randint(keys[2 + 2 * step], (), 0, per_dev)
        value = source_dev * per_dev + jax.random.randint(keys[3 + 2 * step], (), 0, per_dev)
        order = place_value(order, position.astype(jnp.int32), value.astype(jnp.int32))
    return order.astype(jnp.int32)


def place_ends(result, stream_key, low, largest):
    shape = result.shape
    place = [jax.random.randint(jax.random.fold_in(stream_key, axis), (), 0, shape[axis]) for axis in range(len(shape))]
    result = result.at[tuple(place)].set(low)
    longest = shape.index(max(shape))
    place[longest] = (place[longest] + 1) % shape[longest]
    return result.at[tuple(place)].set(largest)


def steps_of(key, dims, cuts, least, largest):
    def one(axis_at, blocks):
        steps = jax.random.uniform(jax.random.fold_in(jax.random.fold_in(key, 6), axis_at), (blocks,), jnp.float32, least / len(cuts), largest / len(cuts))
        return jnp.repeat(jnp.exp(steps), dims[axis_at] // blocks).reshape((-1,) + (1,) * (len(dims) - axis_at - 1))

    gain = one(*cuts[0])
    for cut in cuts[1:]:
        gain = gain * one(*cut)
    return gain


def bell_draw(rng, extent, spread, most, shards=(), kind=jnp.bfloat16):
    drawn = jax.random.normal(rng, extent, jnp.float32) * spread
    if len(shards) > 0:
        drawn = steps_of(rng, extent, shards, -0.22, 0.18) * drawn
    return jnp.clip(drawn, min=-most, max=most).astype(kind)


def setup_inputs(seed: int = 0) -> dict:
    splits = jax.random.split(jax.random.key(seed), 8)
    return {
        "a_blocks": bell_draw(splits[0], (N_ROW, N_COL, SLOTS, BLK, BLK), BLK ** -0.5, 0.3125, ((0, 32), (1, 16))),
        "slot_row": place_ends(jax.random.randint(splits[1], (N_ROW, N_COL, SLOTS), 0, FB_DEV), jax.random.fold_in(splits[1], 1), 0, FB_DEV - 1).astype(jnp.int32),
        "slot_col": place_ends(jax.random.randint(splits[2], (N_ROW, N_COL, SLOTS), 0, CB_DEV), jax.random.fold_in(splits[2], 1), 0, CB_DEV - 1).astype(jnp.int32),
        "slot_count": draw_slot_count(jax.random.fold_in(splits[7], 71), 0),
        "p_blocks": bell_draw(splits[4], (NFB, BLK, BC), 0.25, 1.5, ((0, 32),)),
        "aggregate": place_ends(jax.random.randint(splits[5], (NFB,), 0, NC), jax.random.fold_in(splits[5], 1), 0, NC - 1).astype(jnp.int32),
        "relayout": draw_relayout(jax.random.fold_in(splits[7], 71), 0),
    }


def reference(a_blocks, slot_row, slot_col, slot_count, p_blocks, aggregate, relayout):
    highest = lax.Precision.HIGHEST
    col_blocks = FB_DEV * N_ROW // N_COL
    coarse_ids = jnp.arange(NC, dtype=jnp.int32)
    fine_ids = jnp.arange(FB_DEV, dtype=jnp.int32)
    slot_ids = jnp.arange(SLOTS, dtype=jnp.int32)

    def add_group(total, inputs):
        blocks, slot_rows, slot_cols, live_count, group = inputs
        columns = (jnp.arange(N_COL, dtype=jnp.int32)[:, None] * col_blocks + slot_cols).astype(jnp.int32)
        picked = jnp.take(p_blocks, columns, axis=0).astype(jnp.float32)
        products = jnp.einsum('csab,csbk->csak', blocks.astype(jnp.float32), picked, precision=highest)
        live_slot = slot_ids[None, :] < live_count[:, None]
        row_onehot = ((slot_rows[None, :, :] == fine_ids[:, None, None]) & live_slot[None]).astype(jnp.float32)
        col_onehot = (jnp.take(aggregate, columns)[:, :, None] == coarse_ids[None, None, :]).astype(jnp.float32)
        weights = row_onehot[:, :, :, None] * col_onehot[None]
        applied = jnp.einsum('icsq,csak->iaqk', weights, products, precision=highest)
        first_row = (group * FB_DEV).astype(jnp.int32)
        own_p = lax.dynamic_slice_in_dim(p_blocks, first_row, FB_DEV, 0).astype(jnp.float32)
        projected = jnp.einsum('iam,iaqk->iqmk', own_p, applied, precision=highest)
        own_agg = lax.dynamic_slice_in_dim(aggregate, first_row, FB_DEV, 0)
        agg_onehot = (own_agg[None, :] == coarse_ids[:, None]).astype(jnp.float32)
        return total + jnp.einsum('pi,iqmk->pqmk', agg_onehot, projected, precision=highest), None

    start = jnp.zeros((NC, NC, BC, BC), jnp.float32)
    groups = jnp.arange(N_ROW, dtype=jnp.int32)
    coarse, unused = lax.scan(add_group, start, (a_blocks, slot_row, slot_col, slot_count, groups))
    placed = jnp.take(coarse, relayout, axis=0)
    return placed.transpose(0, 2, 1, 3).reshape(NC, BC, NC * BC)
```

```python
import functools

import jax
import jax.numpy as jnp
from jax import lax
from jax.experimental import pallas as pl
from jax.experimental.pallas import tpu as pltpu
from jax.sharding import PartitionSpec as P

MESH = pl.DeviceIdType.MESH

NX, NY, NZ = 4, 4, 16
TREE = (8, 5, 11, 2, 14)
FAR = (2, 14, 4, 12, 6, 10, 8)
RING = (1, 15, 2, 14, 4, 12, 5, 11, 6, 10, 8)
F32 = jnp.float32
BF16 = jnp.bfloat16


def kernel(
    a_ref, rows_ref, cols_ref, count_ref, p_ref, agg_ref, relay_ref, out_ref,
    a_buf, pt, lhl, p_buf, agg_mine, agg_col, agg_quad, last_vec, col_s, quad_s, last_s, key_s,
    run, d_a, d_b, r_a, r_b, e_a, e_b, r2_a, r2_b, quad, run_z, ob, rz, tile, gat,
    loc_sem, sm_sem, p_ssem, p_rsem, f_ssem, sib_ssem, sib_rsem, ag_ssem, ag_rsem, af_ssem, as_ssem, as_rsem,
    q_ssem, q_rsem, x_ssem, x_rsem, x2_ssem, x2_rsem, z_ssem, z_rsem, w_ssem, w_rsem, o_ssem, o_rsem,
):
    row = lax.axis_index("row")
    col = lax.axis_index("col")
    z, core = row // 2, row % 2
    y, x = col // NX, col % NX
    sib = (z * 2 + 1 - core, col)
    zpair = z + 1 - 2 * (z % 2)
    quad_same = (zpair * 2 + core, col)
    quad_diag = (zpair * 2 + 1 - core, col)

    def at_z(step):
        return (((z + step) % NZ) * 2 + core, col)

    def at_xy(dx, dy):
        return (row, ((y + dy) % NY) * NX + (x + dx) % NX)

    def remote(src, dst, ssem, rsem, dev):
        return pltpu.make_async_remote_copy(
            src_ref=src, dst_ref=dst, send_sem=ssem, recv_sem=rsem, device_id=dev, device_id_type=MESH
        )

    barrier = pltpu.get_barrier_semaphore()
    plane = [(o % NX, o // NX) for o in range(1, NX * NY)]
    partners = [at_z(step) for step in RING] + [at_xy(dx, dy) for dx, dy in plane] + [sib, quad_diag]
    for dev in partners:
        pl.semaphore_signal(barrier, inc=1, device_id=dev, device_id_type=MESH)

    load = pltpu.make_async_copy(a_ref.at[0, 0], a_buf, loc_sem)
    load.start()

    for i in range(4):
        pt[i] = p_ref[i].astype(F32).T.astype(BF16)
    lane8 = lax.broadcasted_iota(jnp.int32, (8, 128), 1)
    mine = jnp.zeros((8, 128), jnp.int32)
    for i in range(4):
        mine = jnp.where(lane8 == i, agg_ref[i], mine)
    agg_mine[...] = mine
    agg_quad[0] = mine
    d = (z + NZ - col) % NZ

    @pl.when(d == 0)
    def _():
        agg_col[core] = mine
        for t in range(2):
            p_buf[core * 2 + t] = jnp.concatenate([p_ref[2 * t], p_ref[2 * t + 1]], axis=1)

    load.wait()

    @pl.loop(0, 16)
    def _(s):
        live = s < count_ref[0, 0]
        left = jnp.dot(pt[rows_ref[0, 0, s]], a_buf[s], preferred_element_type=F32)
        left = jnp.where(live, left, 0.0)
        high = left.astype(BF16)
        lhl[s, 0:64] = high
        lhl[s, 64:128] = (left - high.astype(F32)).astype(BF16)

    pl.semaphore_wait(barrier, len(partners))

    in_tree = d == TREE[0]
    for step in TREE[1:]:
        in_tree = in_tree | (d == step)

    def own_half(t):
        return p_buf.at[core * 2 + t]

    def agg_copy(dev, ssem):
        return remote(agg_col.at[core], agg_col.at[core], ssem, ag_rsem, dev)

    def p_copy(t, dev, ssem):
        return remote(own_half(t), own_half(t), ssem, p_rsem.at[t], dev)

    quad_devs = (sib, quad_same, quad_diag)
    for k in range(3):
        remote(agg_mine, agg_quad.at[k + 1], q_ssem.at[k], q_rsem.at[k], quad_devs[k]).start()

    @pl.when(d == 0)
    def _():
        for k, step in enumerate(TREE):
            agg_copy(at_z(step), ag_ssem.at[k]).start()
        for t in range(2):
            for k, step in enumerate(TREE):
                p_copy(t, at_z(step), p_ssem.at[t, k]).start()

    @pl.when(d != 0)
    def _():
        agg_copy(at_z(1), ag_ssem.at[0]).wait_recv()

    @pl.when(in_tree)
    def _():
        for k, step in enumerate((1, 15)):
            agg_copy(at_z(step), af_ssem.at[k]).start()

    agg_sib = remote(agg_col.at[core], agg_col.at[core], as_ssem, as_rsem, sib)
    agg_sib.start()
    agg_sib_in = remote(agg_col.at[1 - core], agg_col.at[1 - core], as_ssem, as_rsem, sib)
    agg_sib_in.wait_recv()
    to_smem = pltpu.make_async_copy(agg_col, col_s, sm_sem)
    to_smem.start()
    to_smem.wait()

    for s in range(16):
        j = cols_ref[0, 0, s]
        key = rows_ref[0, 0, s] * 32 + col_s[j // 4, 0, j % 4]
        key_s[0, s] = jnp.where(s < count_ref[0, 0], key, -1)
    last = jnp.zeros((8, 128), jnp.int32)
    for s in range(16):
        before = jnp.int32(0)
        for o in range(s):
            before = jnp.where(key_s[0, o] == key_s[0, s], o + 1, before)
        key_s[1, s] = before
        last = jnp.where(lane8 == key_s[0, s], s + 1, last)
    last_vec[...] = last
    to_smem = pltpu.make_async_copy(last_vec, last_s, sm_sem)
    to_smem.start()
    to_smem.wait()

    run[0] = jnp.zeros((64, 128), F32)

    for t in range(2):
        @pl.when(d != 0)
        def _():
            p_copy(t, at_z(1), p_ssem.at[t, 0]).wait_recv()

        @pl.when(in_tree)
        def _():
            for k, step in enumerate((1, 15)):
                p_copy(t, at_z(step), f_ssem.at[t, k]).start()

        remote(own_half(t), own_half(t), sib_ssem.at[t], sib_rsem.at[t], sib).start()
    for t in range(2):
        other = p_buf.at[(1 - core) * 2 + t]
        remote(other, other, sib_ssem.at[t], sib_rsem.at[t], sib).wait_recv()

    lane = lax.broadcasted_iota(jnp.int32, (64, 128), 1)

    @pl.loop(0, 16)
    def _(s):
        j = cols_ref[0, 0, s]
        both = jnp.dot(lhl[s], p_buf[j // 2], preferred_element_type=F32)
        prod = both[0:64] + both[64:128]
        turned = pltpu.roll(prod, 64, 1)
        keep = (lane // 64) == (j % 2)
        run[s + 1] = jnp.where(keep, prod, turned) + run[key_s[1, s]]

    @pl.loop(0, 64)
    def _(t):
        i, yy, xx = t // 16, (t // 4) % 4, t % 4
        base = i * 32 + (t % 16) * 2
        block = jnp.where(lane < 64, run[last_s[0, base]], run[last_s[0, base + 1]])
        d_a[xx, yy, i] = block[0:32]
        d_b[yy, xx, i] = block[32:64]

    first = []
    for k in range(1, 4):
        first.append(remote(d_a.at[(x + k) % NX], r_a.at[k - 1], x_ssem.at[0, k - 1], x_rsem.at[0, k - 1], at_xy(k, 0)))
        first.append(remote(d_b.at[(y + k) % NY], r_b.at[k - 1], x_ssem.at[1, k - 1], x_rsem.at[1, k - 1], at_xy(0, k)))
    for copy in first:
        copy.start()
    for copy in first:
        copy.wait_recv()
    for dense, got, total, here in ((d_a, r_a, e_a, x), (d_b, r_b, e_b, y)):
        @pl.loop(0, 4)
        def _(o):
            total[o] = (dense[here, o] + got[0, o]) + (got[1, o] + got[2, o])

    second = []
    for k in range(1, 4):
        second.append(remote(e_a.at[(y + k) % NY], r2_a.at[k - 1], x2_ssem.at[0, k - 1], x2_rsem.at[0, k - 1], at_xy(0, k)))
        second.append(remote(e_b.at[(x + k) % NX], r2_b.at[k - 1], x2_ssem.at[1, k - 1], x2_rsem.at[1, k - 1], at_xy(k, 0)))
    for copy in second:
        copy.start()
    for copy in second:
        copy.wait_recv()
    quad[0, :, 0:32] = (e_a[y] + r2_a[0]) + (r2_a[1] + r2_a[2])
    quad[0, :, 32:64] = (e_b[x] + r2_b[0]) + (r2_b[1] + r2_b[2])

    to_sib = remote(quad.at[0], quad.at[1], z_ssem.at[0], z_rsem.at[0], sib)
    to_pair = remote(quad.at[0], quad.at[2], z_ssem.at[1], z_rsem.at[1], quad_same)
    on_sib = remote(quad.at[2], quad.at[3], z_ssem.at[2], z_rsem.at[2], sib)
    to_pair.start()
    to_sib.start()

    for k in range(3):
        remote(agg_mine, agg_quad.at[k + 1], q_ssem.at[k], q_rsem.at[k], quad_devs[k]).wait()
    to_smem = pltpu.make_async_copy(agg_quad, quad_s, sm_sem)
    to_smem.start()
    to_smem.wait()
    labels = [quad_s[g // 4, 0, g % 4] for g in range(16)]

    run_z[0] = jnp.zeros((64, 128), F32)

    def chain(group):
        for g in range(group * 4, group * 4 + 4):
            before = jnp.int32(0)
            for o in range(g):
                before = jnp.where(labels[o] == labels[g], o + 1, before)
            run_z[g + 1] = quad[group, g % 4] + run_z[before]

    chain(0)
    to_sib.wait_recv()
    chain(1)
    to_pair.wait_recv()
    on_sib.start()
    chain(2)
    on_sib.wait_recv()
    chain(3)

    far = []
    for k, step in enumerate((0,) + FAR):
        wanted = relay_ref[((z + step) % NZ) * 2 + core]
        at = jnp.int32(0)
        for g in range(16):
            at = jnp.where(labels[g] == wanted, g + 1, at)
        ob[k] = run_z[at]
        if k:
            copy = remote(ob.at[k], rz.at[k - 1], w_ssem.at[k - 1], w_rsem.at[k - 1], at_z(step))
            copy.start()
            far.append(copy)
    total = ob[0]
    for k, copy in enumerate(far):
        copy.wait_recv()
        total = total + rz[k]
    tile[...] = total

    spread = []
    for k, (dx, dy) in enumerate(plane):
        copy = remote(tile, gat.at[k], o_ssem.at[k], o_rsem.at[k], at_xy(dx, dy))
        copy.start()
        spread.append(copy)
    out_ref[0, :, pl.ds(pl.multiple_of(col * 128, 128), 128)] = tile[...]
    for k, (dx, dy) in enumerate(plane):
        spread[k].wait_recv()
        source = ((y + NY - dy) % NY) * NX + (x + NX - dx) % NX
        out_ref[0, :, pl.ds(pl.multiple_of(source * 128, 128), 128)] = gat[k]

    for copy in first + second + [to_sib, to_pair, on_sib] + far + spread + [agg_sib]:
        copy.wait_send()
    for t in range(2):
        remote(own_half(t), own_half(t), sib_ssem.at[t], sib_rsem.at[t], sib).wait_send()

    @pl.when(d == 0)
    def _():
        for k, step in enumerate(TREE):
            agg_copy(at_z(step), ag_ssem.at[k]).wait_send()
            for t in range(2):
                p_copy(t, at_z(step), p_ssem.at[t, k]).wait_send()

    @pl.when(in_tree)
    def _():
        for k, step in enumerate((1, 15)):
            agg_copy(at_z(step), af_ssem.at[k]).wait_send()
            for t in range(2):
                p_copy(t, at_z(step), f_ssem.at[t, k]).wait_send()


def on_device(a_blocks, slot_row, slot_col, slot_count, p_blocks, aggregate, relayout):
    smem = pl.BlockSpec(memory_space=pltpu.SMEM)
    vmem = pl.BlockSpec(memory_space=pltpu.VMEM)
    dma = pltpu.SemaphoreType.DMA
    return pl.pallas_call(
        kernel,
        out_shape=jax.ShapeDtypeStruct((1, 64, 2048), F32),
        in_specs=[pl.BlockSpec(memory_space=pl.ANY), smem, smem, smem, vmem, smem, smem],
        out_specs=vmem,
        scratch_shapes=[
            pltpu.VMEM((16, 320, 320), BF16),
            pltpu.VMEM((4, 64, 320), BF16),
            pltpu.VMEM((16, 128, 320), BF16),
            pltpu.VMEM((4, 320, 128), BF16),
            pltpu.VMEM((8, 128), jnp.int32),
            pltpu.VMEM((2, 8, 128), jnp.int32),
            pltpu.VMEM((4, 8, 128), jnp.int32),
            pltpu.VMEM((8, 128), jnp.int32),
            pltpu.SMEM((2, 8, 128), jnp.int32),
            pltpu.SMEM((4, 8, 128), jnp.int32),
            pltpu.SMEM((8, 128), jnp.int32),
            pltpu.SMEM((2, 16), jnp.int32),
            pltpu.VMEM((17, 64, 128), F32),
            pltpu.VMEM((4, 4, 4, 32, 128), F32),
            pltpu.VMEM((4, 4, 4, 32, 128), F32),
            pltpu.VMEM((3, 4, 4, 32, 128), F32),
            pltpu.VMEM((3, 4, 4, 32, 128), F32),
            pltpu.VMEM((4, 4, 32, 128), F32),
            pltpu.VMEM((4, 4, 32, 128), F32),
            pltpu.VMEM((3, 4, 32, 128), F32),
            pltpu.VMEM((3, 4, 32, 128), F32),
            pltpu.VMEM((4, 4, 64, 128), F32),
            pltpu.VMEM((17, 64, 128), F32),
            pltpu.VMEM((8, 64, 128), F32),
            pltpu.VMEM((7, 64, 128), F32),
            pltpu.VMEM((64, 128), F32),
            pltpu.VMEM((15, 64, 128), F32),
            dma, dma,
            dma((2, 5)), dma((2,)), dma((2, 2)), dma((2,)), dma((2,)),
            dma((5,)), dma, dma((2,)), dma, dma,
            dma((3,)), dma((3,)),
            dma((2, 3)), dma((2, 3)), dma((2, 3)), dma((2, 3)),
            dma((3,)), dma((3,)), dma((7,)), dma((7,)), dma((15,)), dma((15,)),
        ],
        compiler_params=pltpu.CompilerParams(
            collective_id=0, has_side_effects=True, vmem_limit_bytes=40 << 20
        ),
        name="coarse_operator",
    )(a_blocks, slot_row, slot_col, slot_count, p_blocks, aggregate, relayout)


def solution(mesh):
    return jax.shard_map(
        on_device,
        mesh=mesh,
        in_specs=(
            P("row", "col", None, None, None),
            P("row", "col", None),
            P("row", "col", None),
            P("row", "col"),
            P("row", None, None),
            P("row"),
            P(),
        ),
        out_specs=P("row", None, None),
        check_vma=False,
    )
```

```python
import functools

import jax
import jax.numpy as jnp
from jax import lax
from jax.experimental import pallas as pl
from jax.experimental.pallas import tpu as pltpu
from jax.sharding import PartitionSpec as P

MESH = pl.DeviceIdType.MESH

NX, NY, NZ = 4, 4, 16
TREE = (8, 5, 11, 2, 14)
FAR = (2, 14, 4, 12, 6, 10, 8)
RING = (1, 15, 2, 14, 4, 12, 5, 11, 6, 10, 8)
F32 = jnp.float32
BF16 = jnp.bfloat16


def kernel(
    a_hbm, rows_hbm, cols_hbm, count_hbm, p_ref, agg_hbm, relay_hbm, out_ref,
    a_buf, lhl, p_buf, rows_ref, cols_ref, count_ref, agg_ref, relay_ref,
    agg_mine, agg_col, agg_quad, keys_x, keys_y, table, col_s, quad_s, table_s,
    g_a, g_b, run_a, run_b, e_a, e_b, r2_a, r2_b, quad, run_z, ob, rz, tile, gat,
    loc_sem, sm_sem, p_ssem, p_rsem, f_ssem, sib_ssem, sib_rsem, ag_ssem, ag_rsem, af_ssem, as_ssem, as_rsem,
    q_ssem, q_rsem, k_ssem, k_rsem, x_ssem, x_rsem, x2_ssem, x2_rsem, z_ssem, z_rsem, w_ssem, w_rsem, o_ssem, o_rsem,
):
    row = lax.axis_index("row")
    col = lax.axis_index("col")
    z, core = row // 2, row % 2
    y, x = col // NX, col % NX
    sib = (z * 2 + 1 - core, col)
    zpair = z + 1 - 2 * (z % 2)
    quad_same = (zpair * 2 + core, col)
    quad_diag = (zpair * 2 + 1 - core, col)
    pending = []

    def at_z(step):
        return (((z + step) % NZ) * 2 + core, col)

    def at_xy(dx, dy):
        return (row, ((y + dy) % NY) * NX + (x + dx) % NX)

    def remote(src, dst, ssem, rsem, dev):
        return pltpu.make_async_remote_copy(
            src_ref=src, dst_ref=dst, send_sem=ssem, recv_sem=rsem, device_id=dev, device_id_type=MESH
        )

    def start(copy):
        copy.start()
        pending.append(copy.wait_send)
        return copy

    def finish():
        for wait in pending:
            wait()

    barrier = pltpu.get_barrier_semaphore()
    plane = [(o % NX, o // NX) for o in range(1, NX * NY)]
    partners = [at_z(step) for step in RING] + [at_xy(dx, dy) for dx, dy in plane] + [sib, quad_diag]
    for dev in partners:
        pl.semaphore_signal(barrier, inc=1, device_id=dev, device_id_type=MESH)

    small = ((rows_hbm, rows_ref), (cols_hbm, cols_ref), (count_hbm, count_ref), (agg_hbm, agg_ref), (relay_hbm, relay_ref))
    loads = [pltpu.make_async_copy(src, dst, loc_sem.at[k]) for k, (src, dst) in enumerate(small)]
    loads.append(pltpu.make_async_copy(a_hbm.at[0, 0], a_buf, loc_sem.at[5]))
    for load in loads:
        load.start()
    for load in loads[:5]:
        load.wait()

    lane8 = lax.broadcasted_iota(jnp.int32, (8, 128), 1)
    mine = jnp.zeros((8, 128), jnp.int32)
    for i in range(4):
        mine = jnp.where(lane8 == i, agg_ref[i], mine)
    agg_mine[...] = mine
    agg_quad[0] = mine
    d = (z + NZ - col) % NZ

    @pl.when(d == 0)
    def _():
        agg_col[core] = mine
        for t in range(2):
            both = jnp.concatenate([p_ref[2 * t], p_ref[2 * t + 1]], axis=0)
            p_buf[core * 2 + t] = both.astype(F32).T.astype(BF16)

    loads[5].wait()

    @pl.loop(0, 16)
    def _(s):
        live = s < count_ref[0, 0]
        left = jnp.dot(p_ref[rows_ref[0, 0, s]], a_buf[s], preferred_element_type=F32)
        left = jnp.where(live, left, 0.0)
        high = left.astype(BF16)
        lhl[s, 0:64] = high
        lhl[s, 64:128] = (left - high.astype(F32)).astype(BF16)

    pl.semaphore_wait(barrier, len(partners))

    in_tree = d == TREE[0]
    for step in TREE[1:]:
        in_tree = in_tree | (d == step)

    def own_half(t):
        return p_buf.at[core * 2 + t]

    def agg_copy(dev, ssem):
        return remote(agg_col.at[core], agg_col.at[core], ssem, ag_rsem, dev)

    def p_copy(t, dev, ssem):
        return remote(own_half(t), own_half(t), ssem, p_rsem.at[t], dev)

    def start_when(condition, copies):
        @pl.when(condition)
        def _():
            for copy in copies:
                copy.start()

        def wait():
            @pl.when(condition)
            def _():
                for copy in copies:
                    copy.wait_send()

        pending.append(wait)

    quad_devs = (sib, quad_same, quad_diag)
    quad_in = [start(remote(agg_mine, agg_quad.at[k + 1], q_ssem.at[k], q_rsem.at[k], quad_devs[k])) for k in range(3)]
    start_when(d == 0, [agg_copy(at_z(step), ag_ssem.at[k]) for k, step in enumerate(TREE)])
    for t in range(2):
        start_when(d == 0, [p_copy(t, at_z(step), p_ssem.at[t, k]) for k, step in enumerate(TREE)])

    @pl.when(d != 0)
    def _():
        agg_copy(at_z(1), ag_ssem.at[0]).wait_recv()

    start_when(in_tree, [agg_copy(at_z(step), af_ssem.at[k]) for k, step in enumerate((1, 15))])
    start(remote(agg_col.at[core], agg_col.at[core], as_ssem, as_rsem, sib))
    for t in range(2):
        @pl.when(d != 0)
        def _():
            p_copy(t, at_z(1), p_ssem.at[t, 0]).wait_recv()

        start_when(in_tree, [p_copy(t, at_z(step), f_ssem.at[t, k]) for k, step in enumerate((1, 15))])
        start(remote(own_half(t), own_half(t), sib_ssem.at[t], sib_rsem.at[t], sib))

    remote(agg_col.at[1 - core], agg_col.at[1 - core], as_ssem, as_rsem, sib).wait_recv()
    to_smem = pltpu.make_async_copy(agg_col, col_s, sm_sem)
    to_smem.start()
    to_smem.wait()
    for s in range(16):
        j = cols_ref[0, 0, s]
        key = rows_ref[0, 0, s] * 32 + col_s[j // 4, 0, j % 4]
        line = jnp.full((1, 128), jnp.where(s < count_ref[0, 0], key, -1), jnp.int32)
        keys_x[0, s : s + 1] = line
        keys_y[0, s : s + 1] = line
    keys_in = []
    for k in range(1, 4):
        keys_in.append(start(remote(keys_x.at[0], keys_x.at[k], k_ssem.at[0, k - 1], k_rsem.at[0, k - 1], at_xy(k, 0))))
        keys_in.append(start(remote(keys_y.at[0], keys_y.at[k], k_ssem.at[1, k - 1], k_rsem.at[1, k - 1], at_xy(0, k))))

    for t in range(2):
        other = p_buf.at[(1 - core) * 2 + t]
        remote(other, other, sib_ssem.at[t], sib_rsem.at[t], sib).wait_recv()

    lane = lax.broadcasted_iota(jnp.int32, (64, 128), 1)

    def product(s, side):
        j = cols_ref[0, 0, s]
        both = jnp.dot(lhl[s], p_buf[j // 2], preferred_element_type=F32)
        prod = both[0:64] + both[64:128]
        return jnp.where(j % 2 == side, prod, pltpu.roll(prod, 64, 1))

    @pl.loop(0, 8)
    def _(t):
        pair = jnp.where(lane < 64, product(2 * t, 0), product(2 * t + 1, 1))
        g_a[0, t] = pair[0:32]
        g_b[0, t] = pair[32:64]

    first_a, first_b = [], []
    for k in range(1, 4):
        first_a.append(start(remote(g_a.at[0], g_a.at[k], x_ssem.at[0, k - 1], x_rsem.at[0, k - 1], at_xy(k, 0))))
        first_b.append(start(remote(g_b.at[0], g_b.at[k], x_ssem.at[1, k - 1], x_rsem.at[1, k - 1], at_xy(0, k))))

    for copy in keys_in:
        copy.wait_recv()
    lane_i = lax.broadcasted_iota(jnp.int32, (64, 128), 1)
    slot_i = lax.broadcasted_iota(jnp.int32, (64, 128), 0)
    table[...] = jnp.zeros((8, 128), jnp.int32)
    for h, keys in enumerate((keys_x, keys_y)):
        down = keys[...].reshape(64, 128)
        across = jnp.sum(jnp.where(slot_i == lane_i, down, 0), axis=0, keepdims=True)
        before = jnp.where((down == across) & (slot_i < lane_i), slot_i + 1, 0)
        table[2 * h : 2 * h + 1] = jnp.max(before, axis=0, keepdims=True)
        table[2 * h + 1 : 2 * h + 2] = jnp.max(jnp.where(down == lane_i, slot_i + 1, 0), axis=0, keepdims=True)
    to_smem = pltpu.make_async_copy(table, table_s, sm_sem)
    to_smem.start()
    to_smem.wait()

    half_lane = lax.broadcasted_iota(jnp.int32, (32, 128), 1)
    low = half_lane < 64
    run_a[0] = jnp.zeros((32, 128), F32)
    run_b[0] = jnp.zeros((32, 128), F32)
    for k in range(4):
        if k:
            first_a[k - 1].wait_recv()
            first_b[k - 1].wait_recv()

        @pl.loop(0, 8)
        def _(t):
            for h, (got, run) in enumerate(((g_a, run_a), (g_b, run_b))):
                pair = got[k, t]
                turned = pltpu.roll(pair, 64, 1)
                s = k * 16 + 2 * t
                run[s + 1] = jnp.where(low, pair, turned) + run[table_s[2 * h, s]]
                run[s + 2] = jnp.where(low, turned, pair) + run[table_s[2 * h, s + 1]]

    second_a, second_b = [], []
    for k in (1, 2, 3, 0):
        there = (y + k) % NY
        for i in range(4):
            at = i * 32 + (there * NX + x) * 2
            e_a[k, i] = jnp.where(low, run_a[table_s[1, at]], run_a[table_s[1, at + 1]])
        if k:
            second_a.append(start(remote(e_a.at[k], r2_a.at[k - 1], x2_ssem.at[0, k - 1], x2_rsem.at[0, k - 1], at_xy(0, k))))
        there = (x + k) % NX
        for i in range(4):
            at = i * 32 + (y * NX + there) * 2
            e_b[k, i] = jnp.where(low, run_b[table_s[3, at]], run_b[table_s[3, at + 1]])
        if k:
            second_b.append(start(remote(e_b.at[k], r2_b.at[k - 1], x2_ssem.at[1, k - 1], x2_rsem.at[1, k - 1], at_xy(k, 0))))

    to_pair, to_sib, on_sib = [], [], []
    for h, (second, own, got) in enumerate(((second_a, e_a, r2_a), (second_b, e_b, r2_b))):
        for copy in second:
            copy.wait_recv()
        quad[0, h] = (own[0] + got[0]) + (got[1] + got[2])
        to_pair.append(start(remote(quad.at[0, h], quad.at[2, h], z_ssem.at[h, 1], z_rsem.at[h, 1], quad_same)))
        to_sib.append(start(remote(quad.at[0, h], quad.at[1, h], z_ssem.at[h, 0], z_rsem.at[h, 0], sib)))
        on_sib.append(remote(quad.at[2, h], quad.at[3, h], z_ssem.at[h, 2], z_rsem.at[h, 2], sib))

    for copy in quad_in:
        copy.wait_recv()
    to_smem = pltpu.make_async_copy(agg_quad, quad_s, sm_sem)
    to_smem.start()
    to_smem.wait()
    labels = [quad_s[g // 4, 0, g % 4] for g in range(16)]
    previous = []
    for g in range(16):
        before = jnp.int32(0)
        for o in range(g):
            before = jnp.where(labels[o] == labels[g], o + 1, before)
        previous.append(before)
    lasts = []
    for step in (0,) + FAR:
        wanted = relay_ref[((z + step) % NZ) * 2 + core]
        at = jnp.int32(0)
        for g in range(16):
            at = jnp.where(labels[g] == wanted, g + 1, at)
        lasts.append(at)

    def chain(h, group):
        for g in range(group * 4, group * 4 + 4):
            run_z[h, g + 1] = quad[group, h, g % 4] + run_z[h, previous[g]]

    for h in range(2):
        run_z[h, 0] = jnp.zeros((32, 128), F32)
        chain(h, 0)
    for h in range(2):
        to_pair[h].wait_recv()
        start(on_sib[h])
    for h in range(2):
        to_sib[h].wait_recv()
        chain(h, 1)
        chain(h, 2)

    far = ([], [])
    for h in range(2):
        on_sib[h].wait_recv()
        chain(h, 3)
        for k, step in enumerate((0,) + FAR):
            ob[h, k] = run_z[h, lasts[k]]
            if k:
                far[h].append(start(remote(ob.at[h, k], rz.at[h, k - 1], w_ssem.at[h, k - 1], w_rsem.at[h, k - 1], at_z(step))))

    spread = ([], [])
    for h in range(2):
        total = ob[h, 0]
        for k, copy in enumerate(far[h]):
            copy.wait_recv()
            total = total + rz[h, k]
        tile[h] = total
        for k, (dx, dy) in enumerate(plane):
            spread[h].append(start(remote(tile.at[h], gat.at[h, k], o_ssem.at[h, k], o_rsem.at[h, k], at_xy(dx, dy))))
        out_ref[0, 32 * h : 32 * h + 32, pl.ds(pl.multiple_of(col * 128, 128), 128)] = tile[h]
    for h in range(2):
        for k, (dx, dy) in enumerate(plane):
            spread[h][k].wait_recv()
            source = ((y + NY - dy) % NY) * NX + (x + NX - dx) % NX
            out_ref[0, 32 * h : 32 * h + 32, pl.ds(pl.multiple_of(source * 128, 128), 128)] = gat[h, k]
    finish()


def on_device(a_blocks, slot_row, slot_col, slot_count, p_blocks, aggregate, relayout):
    hbm = pl.BlockSpec(memory_space=pltpu.HBM)
    vmem = pl.BlockSpec(memory_space=pltpu.VMEM)
    dma = pltpu.SemaphoreType.DMA
    return pl.pallas_call(
        kernel,
        out_shape=jax.ShapeDtypeStruct((1, 64, 2048), F32),
        in_specs=[hbm, hbm, hbm, hbm, vmem, hbm, hbm],
        out_specs=vmem,
        scratch_shapes=[
            pltpu.VMEM((16, 320, 320), BF16),
            pltpu.VMEM((16, 128, 320), BF16),
            pltpu.VMEM((4, 320, 128), BF16),
            pltpu.SMEM((1, 1, 16), jnp.int32),
            pltpu.SMEM((1, 1, 16), jnp.int32),
            pltpu.SMEM((1, 1), jnp.int32),
            pltpu.SMEM((4,), jnp.int32),
            pltpu.SMEM((32,), jnp.int32),
            pltpu.VMEM((8, 128), jnp.int32),
            pltpu.VMEM((2, 8, 128), jnp.int32),
            pltpu.VMEM((4, 8, 128), jnp.int32),
            pltpu.VMEM((4, 16, 128), jnp.int32),
            pltpu.VMEM((4, 16, 128), jnp.int32),
            pltpu.VMEM((8, 128), jnp.int32),
            pltpu.SMEM((2, 8, 128), jnp.int32),
            pltpu.SMEM((4, 8, 128), jnp.int32),
            pltpu.SMEM((8, 128), jnp.int32),
            pltpu.VMEM((4, 8, 32, 128), F32),
            pltpu.VMEM((4, 8, 32, 128), F32),
            pltpu.VMEM((65, 32, 128), F32),
            pltpu.VMEM((65, 32, 128), F32),
            pltpu.VMEM((4, 4, 32, 128), F32),
            pltpu.VMEM((4, 4, 32, 128), F32),
            pltpu.VMEM((3, 4, 32, 128), F32),
            pltpu.VMEM((3, 4, 32, 128), F32),
            pltpu.VMEM((4, 2, 4, 32, 128), F32),
            pltpu.VMEM((2, 17, 32, 128), F32),
            pltpu.VMEM((2, 8, 32, 128), F32),
            pltpu.VMEM((2, 7, 32, 128), F32),
            pltpu.VMEM((2, 32, 128), F32),
            pltpu.VMEM((2, 15, 32, 128), F32),
            dma((6,)), dma,
            dma((2, 5)), dma((2,)), dma((2, 2)), dma((2,)), dma((2,)),
            dma((5,)), dma, dma((2,)), dma, dma,
            dma((3,)), dma((3,)), dma((2, 3)), dma((2, 3)),
            dma((2, 3)), dma((2, 3)), dma((2, 3)), dma((2, 3)),
            dma((2, 3)), dma((2, 3)), dma((2, 7)), dma((2, 7)), dma((2, 15)), dma((2, 15)),
        ],
        compiler_params=pltpu.CompilerParams(
            collective_id=0, has_side_effects=True, vmem_limit_bytes=60 << 20
        ),
        name="coarse_operator",
    )(a_blocks, slot_row, slot_col, slot_count, jnp.swapaxes(p_blocks, 1, 2), aggregate, relayout)


def solution(mesh):
    return jax.shard_map(
        on_device,
        mesh=mesh,
        in_specs=(
            P("row", "col", None, None, None),
            P("row", "col", None),
            P("row", "col", None),
            P("row", "col"),
            P("row", None, None),
            P("row"),
            P(),
        ),
        out_specs=P("row", None, None),
        check_vma=False,
    )
```

```python
import functools

import jax
import jax.numpy as jnp
from jax import lax
from jax.experimental import pallas as pl
from jax.experimental.pallas import tpu as pltpu
from jax.sharding import PartitionSpec as P

MESH = pl.DeviceIdType.MESH

NX, NY, NZ = 4, 4, 16
TREE = (8, 5, 11, 2, 14)
FAR = (2, 14, 4, 12, 6, 10, 8)
RING = (1, 15, 2, 14, 4, 12, 5, 11, 6, 10, 8)
F32 = jnp.float32
BF16 = jnp.bfloat16


def kernel(
    a_hbm, rows_hbm, cols_hbm, count_hbm, p_ref, agg_hbm, relay_hbm, out_ref,
    a_buf, lhl, p_buf0, p_buf1, rows_ref, cols_ref, count_ref, agg_ref, relay_ref,
    agg_mine, agg_col, agg_quad, keys_x, keys_y, table, col_s, quad_s, table_s,
    g_a, g_b, run_a, run_b, e_a, e_b, r2_a, r2_b, quad, run_z, ob, rz, tile, gat,
    loc_sem, sm_sem, p_ssem, p_rsem, f_ssem, sib_ssem, sib_rsem, ag_ssem, ag_rsem, af_ssem, as_ssem, as_rsem,
    q_ssem, q_rsem, k_ssem, k_rsem, x_ssem, x_rsem, x2_ssem, x2_rsem, z_ssem, z_rsem, w_ssem, w_rsem, o_ssem, o_rsem,
):
    row = lax.axis_index("row")
    col = lax.axis_index("col")
    z, core = row // 2, row % 2
    y, x = col // NX, col % NX
    sib = (z * 2 + 1 - core, col)
    zpair = z + 1 - 2 * (z % 2)
    quad_same = (zpair * 2 + core, col)
    quad_diag = (zpair * 2 + 1 - core, col)
    pending = []
    p_buf = (p_buf0, p_buf1)

    def at_z(step):
        return (((z + step) % NZ) * 2 + core, col)

    def at_xy(dx, dy):
        return (row, ((y + dy) % NY) * NX + (x + dx) % NX)

    def remote(src, dst, ssem, rsem, dev):
        return pltpu.make_async_remote_copy(
            src_ref=src, dst_ref=dst, send_sem=ssem, recv_sem=rsem, device_id=dev, device_id_type=MESH
        )

    def start(copy):
        copy.start()
        pending.append(copy.wait_send)
        return copy

    def finish():
        for wait in pending:
            wait()

    barrier = pltpu.get_barrier_semaphore()
    plane = [(o % NX, o // NX) for o in range(1, NX * NY)]
    partners = [at_z(step) for step in RING] + [at_xy(dx, dy) for dx, dy in plane] + [sib, quad_diag]
    for dev in partners:
        pl.semaphore_signal(barrier, inc=1, device_id=dev, device_id_type=MESH)

    small = ((rows_hbm, rows_ref), (cols_hbm, cols_ref), (count_hbm, count_ref), (agg_hbm, agg_ref), (relay_hbm, relay_ref))
    loads = [pltpu.make_async_copy(src, dst, loc_sem.at[k]) for k, (src, dst) in enumerate(small)]
    loads.append(pltpu.make_async_copy(a_hbm.at[0, 0], a_buf, loc_sem.at[5]))
    for load in loads:
        load.start()
    for load in loads[:5]:
        load.wait()

    lane8 = lax.broadcasted_iota(jnp.int32, (8, 128), 1)
    mine = jnp.zeros((8, 128), jnp.int32)
    for i in range(4):
        mine = jnp.where(lane8 == i, agg_ref[i], mine)
    agg_mine[...] = mine
    agg_quad[0] = mine
    d = (z + NZ - col) % NZ

    @pl.when(d == 0)
    def _():
        agg_col[core] = mine
        for t in range(2):
            both = jnp.concatenate([p_ref[i, 32 * t : 32 * t + 32] for i in range(4)], axis=0)
            p_buf[t][core] = both.astype(F32).T.astype(BF16)

    pl.semaphore_wait(barrier, len(partners))

    in_tree = d == TREE[0]
    for step in TREE[1:]:
        in_tree = in_tree | (d == step)

    def own_half(t):
        return p_buf[t].at[core]

    def agg_copy(dev, ssem):
        return remote(agg_col.at[core], agg_col.at[core], ssem, ag_rsem, dev)

    def p_copy(t, dev, ssem):
        return remote(own_half(t), own_half(t), ssem, p_rsem.at[t], dev)

    def start_when(condition, copies):
        @pl.when(condition)
        def _():
            for copy in copies:
                copy.start()

        def wait():
            @pl.when(condition)
            def _():
                for copy in copies:
                    copy.wait_send()

        pending.append(wait)

    quad_devs = (sib, quad_same, quad_diag)
    quad_in = [start(remote(agg_mine, agg_quad.at[k + 1], q_ssem.at[k], q_rsem.at[k], quad_devs[k])) for k in range(3)]
    start_when(d == 0, [agg_copy(at_z(step), ag_ssem.at[k]) for k, step in enumerate(TREE)])
    for t in range(2):
        start_when(d == 0, [p_copy(t, at_z(step), p_ssem.at[t, k]) for k, step in enumerate(TREE)])

    loads[5].wait()

    @pl.loop(0, 16)
    def _(s):
        live = s < count_ref[0, 0]
        left = jnp.dot(p_ref[rows_ref[0, 0, s]], a_buf[s], preferred_element_type=F32)
        left = jnp.where(live, left, 0.0)
        high = left.astype(BF16)
        lhl[s, 0:64] = high
        lhl[s, 64:128] = (left - high.astype(F32)).astype(BF16)

    @pl.when(d != 0)
    def _():
        agg_copy(at_z(1), ag_ssem.at[0]).wait_recv()

    start_when(in_tree, [agg_copy(at_z(step), af_ssem.at[k]) for k, step in enumerate((1, 15))])
    start(remote(agg_col.at[core], agg_col.at[core], as_ssem, as_rsem, sib))

    remote(agg_col.at[1 - core], agg_col.at[1 - core], as_ssem, as_rsem, sib).wait_recv()
    to_smem = pltpu.make_async_copy(agg_col, col_s, sm_sem)
    to_smem.start()
    to_smem.wait()
    for s in range(16):
        j = cols_ref[0, 0, s]
        key = rows_ref[0, 0, s] * 32 + col_s[j // 4, 0, j % 4]
        line = jnp.full((1, 128), jnp.where(s < count_ref[0, 0], key, -1), jnp.int32)
        keys_x[0, s : s + 1] = line
        keys_y[0, s : s + 1] = line
    keys_in = []
    for k in range(1, 4):
        keys_in.append(start(remote(keys_x.at[0], keys_x.at[k], k_ssem.at[0, k - 1], k_rsem.at[0, k - 1], at_xy(k, 0))))
        keys_in.append(start(remote(keys_y.at[0], keys_y.at[k], k_ssem.at[1, k - 1], k_rsem.at[1, k - 1], at_xy(0, k))))

    group = lax.broadcasted_iota(jnp.int32, (64, 128), 1) // 32
    small_group = lax.broadcasted_iota(jnp.int32, (32, 128), 1) // 32
    low = small_group < 2

    def prolongator_in(t):
        @pl.when(d != 0)
        def _():
            p_copy(t, at_z(1), p_ssem.at[t, 0]).wait_recv()

        start_when(in_tree, [p_copy(t, at_z(step), f_ssem.at[t, k]) for k, step in enumerate((1, 15))])
        start(remote(own_half(t), own_half(t), sib_ssem.at[t], sib_rsem.at[t], sib))
        other = p_buf[t].at[1 - core]
        remote(other, other, sib_ssem.at[t], sib_rsem.at[t], sib).wait_recv()

    def product(t, s, v):
        j = cols_ref[0, 0, s]
        both = jnp.dot(lhl[s], p_buf[t][j // 4], preferred_element_type=F32)
        return pltpu.roll(both[0:64] + both[64:128], ((v + 4 - j % 4) % 4) * 32, 1)

    first_a, first_b = ([], []), ([], [])

    def products_out(t):
        @pl.loop(0, 4)
        def _(u):
            four = product(t, 4 * u, 0)
            for v in range(1, 4):
                four = jnp.where(group == v, product(t, 4 * u + v, v), four)
            g_a[t, 0, u] = four[0:32]
            g_b[t, 0, u] = four[32:64]

        for k in range(1, 4):
            first_a[t].append(start(remote(g_a.at[t, 0], g_a.at[t, k], x_ssem.at[t, 0, k - 1], x_rsem.at[t, 0, k - 1], at_xy(k, 0))))
            first_b[t].append(start(remote(g_b.at[t, 0], g_b.at[t, k], x_ssem.at[t, 1, k - 1], x_rsem.at[t, 1, k - 1], at_xy(0, k))))

    prolongator_in(0)
    products_out(0)

    for copy in keys_in:
        copy.wait_recv()
    lane_i = lax.broadcasted_iota(jnp.int32, (64, 128), 1)
    slot_i = lax.broadcasted_iota(jnp.int32, (64, 128), 0)
    table[...] = jnp.zeros((8, 128), jnp.int32)
    for h, keys in enumerate((keys_x, keys_y)):
        down = keys[...].reshape(64, 128)
        across = jnp.sum(jnp.where(slot_i == lane_i, down, 0), axis=0, keepdims=True)
        before = jnp.where((down == across) & (slot_i < lane_i), slot_i + 1, 0)
        table[2 * h : 2 * h + 1] = jnp.max(before, axis=0, keepdims=True)
        table[2 * h + 1 : 2 * h + 2] = jnp.max(jnp.where(down == lane_i, slot_i + 1, 0), axis=0, keepdims=True)
    to_smem = pltpu.make_async_copy(table, table_s, sm_sem)
    to_smem.start()

    prolongator_in(1)
    products_out(1)
    to_smem.wait()

    run_a[0] = jnp.zeros((32, 128), F32)
    run_b[0] = jnp.zeros((32, 128), F32)
    second_a, second_b = ([], []), ([], [])

    def blocks(run, h, first_key):
        parts = [run[table_s[2 * h + 1, first_key + o]] for o in (0, 1, 32, 33)]
        return jnp.where(
            low, jnp.where(small_group == 0, parts[0], parts[1]), jnp.where(small_group == 2, parts[2], parts[3])
        )

    def sums_out(t):
        for k in range(4):
            if k:
                first_a[t][k - 1].wait_recv()
                first_b[t][k - 1].wait_recv()

            @pl.loop(0, 4)
            def _(u):
                for v in range(4):
                    s = k * 16 + 4 * u + v
                    for h, (got, run) in enumerate(((g_a, run_a), (g_b, run_b))):
                        one = jnp.where(small_group == v, got[t, k, u], 0.0)
                        one = one + pltpu.roll(one, 64, 1)
                        one = one + pltpu.roll(one, 32, 1)
                        run[s + 1] = one + run[table_s[2 * h, s]]

        for k in (1, 2, 3, 0):
            there = ((y + k) % NY) * NX + x
            for n in range(2):
                e_a[t, k, n] = blocks(run_a, 0, n * 64 + there * 2)
            if k:
                second_a[t].append(start(remote(e_a.at[t, k], r2_a.at[t, k - 1], x2_ssem.at[t, 0, k - 1], x2_rsem.at[t, 0, k - 1], at_xy(0, k))))
            there = y * NX + (x + k) % NX
            for n in range(2):
                e_b[t, k, n] = blocks(run_b, 1, n * 64 + there * 2)
            if k:
                second_b[t].append(start(remote(e_b.at[t, k], r2_b.at[t, k - 1], x2_ssem.at[t, 1, k - 1], x2_rsem.at[t, 1, k - 1], at_xy(k, 0))))

    sums_out(0)
    sums_out(1)

    to_pair, to_sib, on_sib = [], [], []
    for h in range(2):
        for copy in second_a[h] + second_b[h]:
            copy.wait_recv()
        for n in range(2):
            top = (e_a[h, 0, n] + r2_a[h, 0, n]) + (r2_a[h, 1, n] + r2_a[h, 2, n])
            bottom = (e_b[h, 0, n] + r2_b[h, 0, n]) + (r2_b[h, 1, n] + r2_b[h, 2, n])
            quad[0, h, 2 * n] = jnp.where(low, top, pltpu.roll(bottom, 64, 1))
            quad[0, h, 2 * n + 1] = jnp.where(low, pltpu.roll(top, 64, 1), bottom)
        to_pair.append(start(remote(quad.at[0, h], quad.at[2, h], z_ssem.at[h, 1], z_rsem.at[h, 1], quad_same)))
        to_sib.append(start(remote(quad.at[0, h], quad.at[1, h], z_ssem.at[h, 0], z_rsem.at[h, 0], sib)))
        on_sib.append(remote(quad.at[2, h], quad.at[3, h], z_ssem.at[h, 2], z_rsem.at[h, 2], sib))

    for copy in quad_in:
        copy.wait_recv()
    to_smem = pltpu.make_async_copy(agg_quad, quad_s, sm_sem)
    to_smem.start()
    to_smem.wait()
    labels = [quad_s[g // 4, 0, g % 4] for g in range(16)]
    previous = []
    for g in range(16):
        before = jnp.int32(0)
        for o in range(g):
            before = jnp.where(labels[o] == labels[g], o + 1, before)
        previous.append(before)
    lasts = []
    for step in (0,) + FAR:
        wanted = relay_ref[((z + step) % NZ) * 2 + core]
        at = jnp.int32(0)
        for g in range(16):
            at = jnp.where(labels[g] == wanted, g + 1, at)
        lasts.append(at)

    def chain(h, group):
        for g in range(group * 4, group * 4 + 4):
            run_z[h, g + 1] = quad[group, h, g % 4] + run_z[h, previous[g]]

    for h in range(2):
        run_z[h, 0] = jnp.zeros((32, 128), F32)
        chain(h, 0)
    for h in range(2):
        to_pair[h].wait_recv()
        start(on_sib[h])
    for h in range(2):
        to_sib[h].wait_recv()
        chain(h, 1)
        chain(h, 2)

    far = ([], [])
    for h in range(2):
        on_sib[h].wait_recv()
        chain(h, 3)
        for k, step in enumerate((0,) + FAR):
            ob[h, k] = run_z[h, lasts[k]]
            if k:
                far[h].append(start(remote(ob.at[h, k], rz.at[h, k - 1], w_ssem.at[h, k - 1], w_rsem.at[h, k - 1], at_z(step))))

    spread = ([], [])
    for h in range(2):
        total = ob[h, 0]
        for k, copy in enumerate(far[h]):
            copy.wait_recv()
            total = total + rz[h, k]
        tile[h] = total
        for k, (dx, dy) in enumerate(plane):
            spread[h].append(start(remote(tile.at[h], gat.at[h, k], o_ssem.at[h, k], o_rsem.at[h, k], at_xy(dx, dy))))

    def place(source, first, second):
        there = pl.ds(pl.multiple_of(source * 128, 128), 128)
        out_ref[0, 0:32, there] = jnp.where(
            low,
            jnp.where(small_group == 0, first, pltpu.roll(second, 32, 1)),
            jnp.where(small_group == 2, pltpu.roll(first, 32, 1), pltpu.roll(second, 64, 1)),
        )
        out_ref[0, 32:64, there] = jnp.where(
            low,
            jnp.where(small_group == 0, pltpu.roll(first, 64, 1), pltpu.roll(second, 96, 1)),
            jnp.where(small_group == 2, pltpu.roll(first, 96, 1), second),
        )

    place(col, tile[0], tile[1])
    for copy in spread[0]:
        copy.wait_recv()
    for k, (dx, dy) in enumerate(plane):
        spread[1][k].wait_recv()
        source = ((y + NY - dy) % NY) * NX + (x + NX - dx) % NX
        place(source, gat[0, k], gat[1, k])
    finish()


def on_device(a_blocks, slot_row, slot_col, slot_count, p_blocks, aggregate, relayout):
    hbm = pl.BlockSpec(memory_space=pltpu.HBM)
    vmem = pl.BlockSpec(memory_space=pltpu.VMEM)
    dma = pltpu.SemaphoreType.DMA
    return pl.pallas_call(
        kernel,
        out_shape=pltpu.VMEM((1, 64, 2048), F32),
        in_specs=[hbm, hbm, hbm, hbm, vmem, hbm, hbm],
        out_specs=vmem,
        scratch_shapes=[
            pltpu.VMEM((16, 320, 320), BF16),
            pltpu.VMEM((16, 128, 320), BF16),
            pltpu.VMEM((2, 320, 128), BF16),
            pltpu.VMEM((2, 320, 128), BF16),
            pltpu.SMEM((1, 1, 16), jnp.int32),
            pltpu.SMEM((1, 1, 16), jnp.int32),
            pltpu.SMEM((1, 1), jnp.int32),
            pltpu.SMEM((4,), jnp.int32),
            pltpu.SMEM((32,), jnp.int32),
            pltpu.VMEM((8, 128), jnp.int32),
            pltpu.VMEM((2, 8, 128), jnp.int32),
            pltpu.VMEM((4, 8, 128), jnp.int32),
            pltpu.VMEM((4, 16, 128), jnp.int32),
            pltpu.VMEM((4, 16, 128), jnp.int32),
            pltpu.VMEM((8, 128), jnp.int32),
            pltpu.SMEM((2, 8, 128), jnp.int32),
            pltpu.SMEM((4, 8, 128), jnp.int32),
            pltpu.SMEM((8, 128), jnp.int32),
            pltpu.VMEM((2, 4, 4, 32, 128), F32),
            pltpu.VMEM((2, 4, 4, 32, 128), F32),
            pltpu.VMEM((65, 32, 128), F32),
            pltpu.VMEM((65, 32, 128), F32),
            pltpu.VMEM((2, 4, 2, 32, 128), F32),
            pltpu.VMEM((2, 4, 2, 32, 128), F32),
            pltpu.VMEM((2, 3, 2, 32, 128), F32),
            pltpu.VMEM((2, 3, 2, 32, 128), F32),
            pltpu.VMEM((4, 2, 4, 32, 128), F32),
            pltpu.VMEM((2, 17, 32, 128), F32),
            pltpu.VMEM((2, 8, 32, 128), F32),
            pltpu.VMEM((2, 7, 32, 128), F32),
            pltpu.VMEM((2, 32, 128), F32),
            pltpu.VMEM((2, 15, 32, 128), F32),
            dma((6,)), dma,
            dma((2, 5)), dma((2,)), dma((2, 2)), dma((2,)), dma((2,)),
            dma((5,)), dma, dma((2,)), dma, dma,
            dma((3,)), dma((3,)), dma((2, 3)), dma((2, 3)),
            dma((2, 2, 3)), dma((2, 2, 3)), dma((2, 2, 3)), dma((2, 2, 3)),
            dma((2, 3)), dma((2, 3)), dma((2, 7)), dma((2, 7)), dma((2, 15)), dma((2, 15)),
        ],
        compiler_params=pltpu.CompilerParams(
            collective_id=0, has_side_effects=True, vmem_limit_bytes=60 << 20
        ),
        name="coarse_operator",
    )(a_blocks, slot_row, slot_col, slot_count, jnp.swapaxes(p_blocks, 1, 2), aggregate, relayout)


def solution(mesh):
    return jax.shard_map(
        on_device,
        mesh=mesh,
        in_specs=(
            P("row", "col", None, None, None),
            P("row", "col", None),
            P("row", "col", None),
            P("row", "col"),
            P("row", None, None),
            P("row"),
            P(),
        ),
        out_specs=P("row", None, None),
        check_vma=False,
    )
```

```python
import functools

import jax
import jax.numpy as jnp
from jax import lax
from jax.experimental import pallas as pl
from jax.experimental.pallas import tpu as pltpu
from jax.sharding import PartitionSpec as P

MESH = pl.DeviceIdType.MESH

NX, NY, NZ = 4, 4, 16
TREE = (6, 10, 2, 14)
FAR = (2, 14, 4, 12, 6, 10, 8)
RING = (1, 15, 2, 14, 4, 12, 6, 10, 8)
F32 = jnp.float32
BF16 = jnp.bfloat16


def kernel(
    a_hbm, rows_hbm, cols_hbm, count_hbm, p_ref, agg_hbm, relay_hbm, out_ref,
    a_buf, lhl, p_buf0, p_buf1, rows_ref, cols_ref, count_ref, agg_ref, relay_ref,
    agg_mine, agg_col, agg_quad, keys_x, keys_y, table, col_s, quad_s, table_s,
    g_a, g_b, run_a, run_b, e_a, e_b, r2_a, r2_b, quad, run_z, ob, rz, tile, gat,
    loc_sem, sm_sem, p_ssem, p_rsem, f_ssem, sib_ssem, sib_rsem, ag_ssem, ag_rsem, af_ssem, as_ssem, as_rsem,
    q_ssem, q_rsem, k_ssem, k_rsem, x_ssem, x_rsem, x2_ssem, x2_rsem, z_ssem, z_rsem, w_ssem, w_rsem, o_ssem, o_rsem,
):
    row = lax.axis_index("row")
    col = lax.axis_index("col")
    z, core = row // 2, row % 2
    y, x = col // NX, col % NX
    sib = (z * 2 + 1 - core, col)
    zpair = z + 1 - 2 * (z % 2)
    quad_same = (zpair * 2 + core, col)
    quad_diag = (zpair * 2 + 1 - core, col)
    pending = []
    p_buf = (p_buf0, p_buf1)

    def at_z(step):
        return (((z + step) % NZ) * 2 + core, col)

    def at_xy(dx, dy):
        return (row, ((y + dy) % NY) * NX + (x + dx) % NX)

    def remote(src, dst, ssem, rsem, dev):
        return pltpu.make_async_remote_copy(
            src_ref=src, dst_ref=dst, send_sem=ssem, recv_sem=rsem, device_id=dev, device_id_type=MESH
        )

    def start(copy):
        copy.start()
        pending.append(copy.wait_send)
        return copy

    def finish():
        for wait in pending:
            wait()

    barrier = pltpu.get_barrier_semaphore()
    plane = [(o % NX, o // NX) for o in range(1, NX * NY)]
    partners = [at_z(step) for step in RING] + [at_xy(dx, dy) for dx, dy in plane] + [sib, quad_diag]
    for dev in partners:
        pl.semaphore_signal(barrier, inc=1, device_id=dev, device_id_type=MESH)

    small = ((rows_hbm, rows_ref), (cols_hbm, cols_ref), (count_hbm, count_ref), (agg_hbm, agg_ref), (relay_hbm, relay_ref))
    loads = [pltpu.make_async_copy(src, dst, loc_sem.at[k]) for k, (src, dst) in enumerate(small)]
    loads.append(pltpu.make_async_copy(a_hbm.at[0, 0], a_buf, loc_sem.at[5]))
    for load in loads:
        load.start()
    for load in loads[:5]:
        load.wait()

    lane8 = lax.broadcasted_iota(jnp.int32, (8, 128), 1)
    mine = jnp.zeros((8, 128), jnp.int32)
    for i in range(4):
        mine = jnp.where(lane8 == i, agg_ref[i], mine)
    agg_mine[...] = mine
    agg_quad[0] = mine
    d = (z + NZ - col) % NZ

    @pl.when(d == 0)
    def _():
        agg_col[core] = mine
        for t in range(2):
            both = jnp.concatenate([p_ref[i, 32 * t : 32 * t + 32] for i in range(4)], axis=0)
            p_buf[t][core] = both.astype(F32).T.astype(BF16)

    pl.semaphore_wait(barrier, len(partners))

    in_tree = d == TREE[0]
    for step in TREE[1:]:
        in_tree = in_tree | (d == step)

    def own_half(t):
        return p_buf[t].at[core]

    def agg_copy(dev, ssem):
        return remote(agg_col.at[core], agg_col.at[core], ssem, ag_rsem, dev)

    def p_copy(t, dev, ssem):
        return remote(own_half(t), own_half(t), ssem, p_rsem.at[t], dev)

    def start_when(condition, copies):
        @pl.when(condition)
        def _():
            for copy in copies:
                copy.start()

        def wait():
            @pl.when(condition)
            def _():
                for copy in copies:
                    copy.wait_send()

        pending.append(wait)

    def pass_on(copy_to):
        start_when((d == 6) | (d == 10), [copy_to(2, 0)])
        start_when(d == 6, [copy_to(14, 1)])
        start_when(in_tree, [copy_to(1, 2), copy_to(15, 3)])

    quad_devs = (sib, quad_same, quad_diag)
    quad_in = [start(remote(agg_mine, agg_quad.at[k + 1], q_ssem.at[k], q_rsem.at[k], quad_devs[k])) for k in range(3)]
    start_when(d == 0, [agg_copy(at_z(step), ag_ssem.at[k]) for k, step in enumerate(TREE)])
    p_out = [[p_copy(t, at_z(step), p_ssem.at[t, k]) for k, step in enumerate(TREE)] for t in range(2)]

    @pl.when(d == 0)
    def _():
        for copy in p_out[0]:
            copy.start()

    loads[5].wait()

    @pl.loop(0, 16)
    def _(s):
        live = s < count_ref[0, 0]
        left = jnp.dot(p_ref[rows_ref[0, 0, s]], a_buf[s], preferred_element_type=F32)
        left = jnp.where(live, left, 0.0)
        high = left.astype(BF16)
        lhl[s, 0:64] = high
        lhl[s, 64:128] = (left - high.astype(F32)).astype(BF16)

    @pl.when(d == 0)
    def _():
        for copy in p_out[0]:
            copy.wait_send()

    start_when(d == 0, p_out[1])

    @pl.when(d != 0)
    def _():
        agg_copy(at_z(1), ag_ssem.at[0]).wait_recv()

    pass_on(lambda step, k: agg_copy(at_z(step), af_ssem.at[k]))
    start(remote(agg_col.at[core], agg_col.at[core], as_ssem, as_rsem, sib))

    keys_in = []
    for k in range(1, 4):
        keys_in.append(remote(keys_x.at[0], keys_x.at[k], k_ssem.at[0, k - 1], k_rsem.at[0, k - 1], at_xy(k, 0)))
        keys_in.append(remote(keys_y.at[0], keys_y.at[k], k_ssem.at[1, k - 1], k_rsem.at[1, k - 1], at_xy(0, k)))
    for copy in keys_in:
        pending.append(copy.wait_send)

    def keys_out():
        remote(agg_col.at[1 - core], agg_col.at[1 - core], as_ssem, as_rsem, sib).wait_recv()
        to_smem = pltpu.make_async_copy(agg_col, col_s, sm_sem)
        to_smem.start()
        to_smem.wait()
        for s in range(16):
            j = cols_ref[0, 0, s]
            key = rows_ref[0, 0, s] * 32 + col_s[j // 4, 0, j % 4]
            line = jnp.full((1, 128), jnp.where(s < count_ref[0, 0], key, -1), jnp.int32)
            keys_x[0, s : s + 1] = line
            keys_y[0, s : s + 1] = line
        for copy in keys_in:
            copy.start()

    outside = (d != 0) & jnp.logical_not(in_tree)

    @pl.when(jnp.logical_not(in_tree))
    def _():
        keys_out()

    @pl.when(d != 0)
    def _():
        p_copy(0, at_z(1), p_ssem.at[0, 0]).wait_recv()

    pass_on(lambda step, k: p_copy(0, at_z(step), f_ssem.at[0, k]))
    start(remote(own_half(0), own_half(0), sib_ssem.at[0], sib_rsem.at[0], sib))

    @pl.when(in_tree)
    def _():
        p_copy(1, at_z(1), p_ssem.at[1, 0]).wait_recv()

    pass_on(lambda step, k: p_copy(1, at_z(step), f_ssem.at[1, k]))

    @pl.when(in_tree)
    def _():
        keys_out()

    def sibling_in(t):
        other = p_buf[t].at[1 - core]
        remote(other, other, sib_ssem.at[t], sib_rsem.at[t], sib).wait_recv()

    group = lax.broadcasted_iota(jnp.int32, (64, 128), 1) // 32
    small_group = lax.broadcasted_iota(jnp.int32, (32, 128), 1) // 32
    low = small_group < 2

    def product(t, s, v):
        j = cols_ref[0, 0, s]
        both = jnp.dot(lhl[s], p_buf[t][j // 4], preferred_element_type=F32)
        return pltpu.roll(both[0:64] + both[64:128], ((v + 4 - j % 4) % 4) * 32, 1)

    first_a, first_b = ([], []), ([], [])

    def products_out(t):
        @pl.loop(0, 4)
        def _(u):
            four = product(t, 4 * u, 0)
            for v in range(1, 4):
                four = jnp.where(group == v, product(t, 4 * u + v, v), four)
            g_a[t, 0, u] = four[0:32]
            g_b[t, 0, u] = four[32:64]

        for k in range(1, 4):
            first_a[t].append(start(remote(g_a.at[t, 0], g_a.at[t, k], x_ssem.at[t, 0, k - 1], x_rsem.at[t, 0, k - 1], at_xy(k, 0))))
            first_b[t].append(start(remote(g_b.at[t, 0], g_b.at[t, k], x_ssem.at[t, 1, k - 1], x_rsem.at[t, 1, k - 1], at_xy(0, k))))

    sibling_in(0)
    products_out(0)

    @pl.when(outside)
    def _():
        p_copy(1, at_z(1), p_ssem.at[1, 0]).wait_recv()

    start(remote(own_half(1), own_half(1), sib_ssem.at[1], sib_rsem.at[1], sib))

    for copy in keys_in:
        copy.wait_recv()
    lane_i = lax.broadcasted_iota(jnp.int32, (64, 128), 1)
    slot_i = lax.broadcasted_iota(jnp.int32, (64, 128), 0)
    table[...] = jnp.zeros((8, 128), jnp.int32)
    for h, keys in enumerate((keys_x, keys_y)):
        down = keys[...].reshape(64, 128)
        across = jnp.sum(jnp.where(slot_i == lane_i, down, 0), axis=0, keepdims=True)
        before = jnp.where((down == across) & (slot_i < lane_i), slot_i + 1, 0)
        table[2 * h : 2 * h + 1] = jnp.max(before, axis=0, keepdims=True)
        table[2 * h + 1 : 2 * h + 2] = jnp.max(jnp.where(down == lane_i, slot_i + 1, 0), axis=0, keepdims=True)
    to_smem = pltpu.make_async_copy(table, table_s, sm_sem)
    to_smem.start()

    sibling_in(1)
    products_out(1)
    to_smem.wait()

    run_a[0] = jnp.zeros((32, 128), F32)
    run_b[0] = jnp.zeros((32, 128), F32)
    second_a, second_b = ([], []), ([], [])

    def blocks(run, h, first_key):
        parts = [run[table_s[2 * h + 1, first_key + o]] for o in (0, 1, 32, 33)]
        return jnp.where(
            low, jnp.where(small_group == 0, parts[0], parts[1]), jnp.where(small_group == 2, parts[2], parts[3])
        )

    def sums_out(t):
        for k in range(4):
            if k:
                first_a[t][k - 1].wait_recv()
                first_b[t][k - 1].wait_recv()

            @pl.loop(0, 4)
            def _(u):
                for v in range(4):
                    s = k * 16 + 4 * u + v
                    for h, (got, run) in enumerate(((g_a, run_a), (g_b, run_b))):
                        one = jnp.where(small_group == v, got[t, k, u], 0.0)
                        one = one + pltpu.roll(one, 64, 1)
                        one = one + pltpu.roll(one, 32, 1)
                        run[s + 1] = one + run[table_s[2 * h, s]]

        for k in (1, 2, 3, 0):
            there = ((y + k) % NY) * NX + x
            for n in range(2):
                e_a[t, k, n] = blocks(run_a, 0, n * 64 + there * 2)
            if k:
                second_a[t].append(start(remote(e_a.at[t, k], r2_a.at[t, k - 1], x2_ssem.at[t, 0, k - 1], x2_rsem.at[t, 0, k - 1], at_xy(0, k))))
            there = y * NX + (x + k) % NX
            for n in range(2):
                e_b[t, k, n] = blocks(run_b, 1, n * 64 + there * 2)
            if k:
                second_b[t].append(start(remote(e_b.at[t, k], r2_b.at[t, k - 1], x2_ssem.at[t, 1, k - 1], x2_rsem.at[t, 1, k - 1], at_xy(k, 0))))

    sums_out(0)
    sums_out(1)

    to_pair, to_sib, on_sib = [], [], []
    for h in range(2):
        for copy in second_a[h] + second_b[h]:
            copy.wait_recv()
        for n in range(2):
            top = (e_a[h, 0, n] + r2_a[h, 0, n]) + (r2_a[h, 1, n] + r2_a[h, 2, n])
            bottom = (e_b[h, 0, n] + r2_b[h, 0, n]) + (r2_b[h, 1, n] + r2_b[h, 2, n])
            quad[0, h, 2 * n] = jnp.where(low, top, pltpu.roll(bottom, 64, 1))
            quad[0, h, 2 * n + 1] = jnp.where(low, pltpu.roll(top, 64, 1), bottom)
        to_pair.append(start(remote(quad.at[0, h], quad.at[2, h], z_ssem.at[h, 1], z_rsem.at[h, 1], quad_same)))
        to_sib.append(start(remote(quad.at[0, h], quad.at[1, h], z_ssem.at[h, 0], z_rsem.at[h, 0], sib)))
        on_sib.append(remote(quad.at[2, h], quad.at[3, h], z_ssem.at[h, 2], z_rsem.at[h, 2], sib))

    for copy in quad_in:
        copy.wait_recv()
    to_smem = pltpu.make_async_copy(agg_quad, quad_s, sm_sem)
    to_smem.start()
    to_smem.wait()
    labels = [quad_s[g // 4, 0, g % 4] for g in range(16)]
    previous = []
    for g in range(16):
        before = jnp.int32(0)
        for o in range(g):
            before = jnp.where(labels[o] == labels[g], o + 1, before)
        previous.append(before)
    lasts = []
    for step in (0,) + FAR:
        wanted = relay_ref[((z + step) % NZ) * 2 + core]
        at = jnp.int32(0)
        for g in range(16):
            at = jnp.where(labels[g] == wanted, g + 1, at)
        lasts.append(at)

    def chain(h, group):
        for g in range(group * 4, group * 4 + 4):
            run_z[h, g + 1] = quad[group, h, g % 4] + run_z[h, previous[g]]

    for h in range(2):
        run_z[h, 0] = jnp.zeros((32, 128), F32)
        chain(h, 0)
    for h in range(2):
        to_pair[h].wait_recv()
        start(on_sib[h])
    for h in range(2):
        to_sib[h].wait_recv()
        chain(h, 1)
        chain(h, 2)

    far = ([], [])
    for h in range(2):
        on_sib[h].wait_recv()
        chain(h, 3)
        for k, step in enumerate((0,) + FAR):
            ob[h, k] = run_z[h, lasts[k]]
            if k:
                far[h].append(start(remote(ob.at[h, k], rz.at[h, k - 1], w_ssem.at[h, k - 1], w_rsem.at[h, k - 1], at_z(step))))

    spread = ([], [])
    for h in range(2):
        total = ob[h, 0]
        for k, copy in enumerate(far[h]):
            copy.wait_recv()
            total = total + rz[h, k]
        tile[h] = total
        for k, (dx, dy) in enumerate(plane):
            spread[h].append(start(remote(tile.at[h], gat.at[h, k], o_ssem.at[h, k], o_rsem.at[h, k], at_xy(dx, dy))))

    def place(source, first, second):
        there = pl.ds(pl.multiple_of(source * 128, 128), 128)
        out_ref[0, 0:32, there] = jnp.where(
            low,
            jnp.where(small_group == 0, first, pltpu.roll(second, 32, 1)),
            jnp.where(small_group == 2, pltpu.roll(first, 32, 1), pltpu.roll(second, 64, 1)),
        )
        out_ref[0, 32:64, there] = jnp.where(
            low,
            jnp.where(small_group == 0, pltpu.roll(first, 64, 1), pltpu.roll(second, 96, 1)),
            jnp.where(small_group == 2, pltpu.roll(first, 96, 1), second),
        )

    place(col, tile[0], tile[1])
    for copy in spread[0]:
        copy.wait_recv()
    for k, (dx, dy) in enumerate(plane):
        spread[1][k].wait_recv()
        source = ((y + NY - dy) % NY) * NX + (x + NX - dx) % NX
        place(source, gat[0, k], gat[1, k])
    finish()


def on_device(a_blocks, slot_row, slot_col, slot_count, p_blocks, aggregate, relayout):
    hbm = pl.BlockSpec(memory_space=pltpu.HBM)
    vmem = pl.BlockSpec(memory_space=pltpu.VMEM)
    dma = pltpu.SemaphoreType.DMA
    return pl.pallas_call(
        kernel,
        out_shape=pltpu.VMEM((1, 64, 2048), F32),
        in_specs=[hbm, hbm, hbm, hbm, vmem, hbm, hbm],
        out_specs=vmem,
        scratch_shapes=[
            pltpu.VMEM((16, 320, 320), BF16),
            pltpu.VMEM((16, 128, 320), BF16),
            pltpu.VMEM((2, 320, 128), BF16),
            pltpu.VMEM((2, 320, 128), BF16),
            pltpu.SMEM((1, 1, 16), jnp.int32),
            pltpu.SMEM((1, 1, 16), jnp.int32),
            pltpu.SMEM((1, 1), jnp.int32),
            pltpu.SMEM((4,), jnp.int32),
            pltpu.SMEM((32,), jnp.int32),
            pltpu.VMEM((8, 128), jnp.int32),
            pltpu.VMEM((2, 8, 128), jnp.int32),
            pltpu.VMEM((4, 8, 128), jnp.int32),
            pltpu.VMEM((4, 16, 128), jnp.int32),
            pltpu.VMEM((4, 16, 128), jnp.int32),
            pltpu.VMEM((8, 128), jnp.int32),
            pltpu.SMEM((2, 8, 128), jnp.int32),
            pltpu.SMEM((4, 8, 128), jnp.int32),
            pltpu.SMEM((8, 128), jnp.int32),
            pltpu.VMEM((2, 4, 4, 32, 128), F32),
            pltpu.VMEM((2, 4, 4, 32, 128), F32),
            pltpu.VMEM((65, 32, 128), F32),
            pltpu.VMEM((65, 32, 128), F32),
            pltpu.VMEM((2, 4, 2, 32, 128), F32),
            pltpu.VMEM((2, 4, 2, 32, 128), F32),
            pltpu.VMEM((2, 3, 2, 32, 128), F32),
            pltpu.VMEM((2, 3, 2, 32, 128), F32),
            pltpu.VMEM((4, 2, 4, 32, 128), F32),
            pltpu.VMEM((2, 17, 32, 128), F32),
            pltpu.VMEM((2, 8, 32, 128), F32),
            pltpu.VMEM((2, 7, 32, 128), F32),
            pltpu.VMEM((2, 32, 128), F32),
            pltpu.VMEM((2, 15, 32, 128), F32),
            dma((6,)), dma,
            dma((2, 4)), dma((2,)), dma((2, 4)), dma((2,)), dma((2,)),
            dma((4,)), dma, dma((4,)), dma, dma,
            dma((3,)), dma((3,)), dma((2, 3)), dma((2, 3)),
            dma((2, 2, 3)), dma((2, 2, 3)), dma((2, 2, 3)), dma((2, 2, 3)),
            dma((2, 3)), dma((2, 3)), dma((2, 7)), dma((2, 7)), dma((2, 15)), dma((2, 15)),
        ],
        compiler_params=pltpu.CompilerParams(
            collective_id=0, has_side_effects=True, vmem_limit_bytes=60 << 20
        ),
        name="coarse_operator",
    )(a_blocks, slot_row, slot_col, slot_count, jnp.swapaxes(p_blocks, 1, 2), aggregate, relayout)


def solution(mesh):
    return jax.shard_map(
        on_device,
        mesh=mesh,
        in_specs=(
            P("row", "col", None, None, None),
            P("row", "col", None),
            P("row", "col", None),
            P("row", "col"),
            P("row", None, None),
            P("row"),
            P(),
        ),
        out_specs=P("row", None, None),
        check_vma=False,
    )
```

```python
import functools

import jax
import jax.numpy as jnp
from jax import lax
from jax.experimental import pallas as pl
from jax.experimental.pallas import tpu as pltpu
from jax.sharding import PartitionSpec as P

MESH = pl.DeviceIdType.MESH

NX, NY, NZ = 4, 4, 16
TREE = (6, 10, 2, 14)
FAR = (8, 6, 10, 4, 12, 2, 14)
RING = (1, 15, 2, 14, 4, 12, 6, 10, 8)
STEPS = 32767.0
F32 = jnp.float32
BF16 = jnp.bfloat16


def kernel(
    a_hbm, rows_hbm, cols_hbm, count_hbm, p_ref, agg_hbm, relay_hbm, out_ref,
    a_buf, lhl, p_buf0, p_buf1, rows_ref, cols_ref, count_ref, agg_ref, relay_ref,
    agg_mine, agg_col, agg_quad, keys_x, keys_y, table, col_s, quad_s, table_s, rows_s,
    g_a, g_b, run_a, run_b, e_a, e_b, r2_a, r2_b, quad, run_z, own, ob, rz, scale, scale_in, tile, gat,
    loc_sem, sm_sem, p_ssem, p_rsem, f_ssem, sib_ssem, sib_rsem, ag_ssem, ag_rsem, af_ssem, as_ssem, as_rsem,
    q_ssem, q_rsem, k_ssem, k_rsem, x_ssem, x_rsem, x2_ssem, x2_rsem, z_ssem, z_rsem, w_ssem, w_rsem, v_ssem, v_rsem, o_ssem, o_rsem,
):
    row = lax.axis_index("row")
    col = lax.axis_index("col")
    z, core = row // 2, row % 2
    y, x = col // NX, col % NX
    sib = (z * 2 + 1 - core, col)
    zpair = z + 1 - 2 * (z % 2)
    quad_same = (zpair * 2 + core, col)
    quad_diag = (zpair * 2 + 1 - core, col)
    pending = []
    p_buf = (p_buf0, p_buf1)

    def at_z(step):
        return (((z + step) % NZ) * 2 + core, col)

    def at_xy(dx, dy):
        return (row, ((y + dy) % NY) * NX + (x + dx) % NX)

    def remote(src, dst, ssem, rsem, dev):
        return pltpu.make_async_remote_copy(
            src_ref=src, dst_ref=dst, send_sem=ssem, recv_sem=rsem, device_id=dev, device_id_type=MESH
        )

    def start(copy):
        copy.start()
        pending.append(copy.wait_send)
        return copy

    def finish():
        for wait in pending:
            wait()

    barrier = pltpu.get_barrier_semaphore()
    plane = sorted(((o % NX, o // NX) for o in range(1, NX * NY)), key=lambda o: -min(o[0], NX - o[0]) - min(o[1], NY - o[1]))
    partners = [at_z(step) for step in RING] + [at_xy(dx, dy) for dx, dy in plane] + [sib, quad_diag]
    for dev in partners:
        pl.semaphore_signal(barrier, inc=1, device_id=dev, device_id_type=MESH)

    small = ((rows_hbm, rows_ref), (cols_hbm, cols_ref), (count_hbm, count_ref), (agg_hbm, agg_ref), (relay_hbm, relay_ref))
    loads = [pltpu.make_async_copy(src, dst, loc_sem.at[k]) for k, (src, dst) in enumerate(small)]
    loads.append(pltpu.make_async_copy(a_hbm.at[0, 0], a_buf, loc_sem.at[5]))
    for load in loads:
        load.start()
    for load in loads[:5]:
        load.wait()

    lane8 = lax.broadcasted_iota(jnp.int32, (8, 128), 1)
    mine = jnp.zeros((8, 128), jnp.int32)
    for i in range(4):
        mine = jnp.where(lane8 == i, agg_ref[i], mine)
    agg_mine[...] = mine
    agg_quad[0] = mine
    d = (z + NZ - col) % NZ

    @pl.when(d == 0)
    def _():
        agg_col[core] = mine
        for t in range(2):
            both = jnp.concatenate([p_ref[i, 32 * t : 32 * t + 32] for i in range(4)], axis=0)
            p_buf[t][core] = both.astype(F32).T.astype(BF16)

    pl.semaphore_wait(barrier, len(partners))

    in_tree = d == TREE[0]
    for step in TREE[1:]:
        in_tree = in_tree | (d == step)

    def own_half(t):
        return p_buf[t].at[core]

    def agg_copy(dev, ssem):
        return remote(agg_col.at[core], agg_col.at[core], ssem, ag_rsem, dev)

    def p_copy(t, dev, ssem):
        return remote(own_half(t), own_half(t), ssem, p_rsem.at[t], dev)

    def start_when(condition, copies):
        @pl.when(condition)
        def _():
            for copy in copies:
                copy.start()

        def wait():
            @pl.when(condition)
            def _():
                for copy in copies:
                    copy.wait_send()

        pending.append(wait)

    def pass_on(copy_to):
        start_when((d == 6) | (d == 10), [copy_to(2, 0)])
        start_when(d == 6, [copy_to(14, 1)])
        start_when(in_tree, [copy_to(1, 2), copy_to(15, 3)])

    quad_devs = (sib, quad_same, quad_diag)
    quad_in = [start(remote(agg_mine, agg_quad.at[k + 1], q_ssem.at[k], q_rsem.at[k], quad_devs[k])) for k in range(3)]
    start_when(d == 0, [agg_copy(at_z(step), ag_ssem.at[k]) for k, step in enumerate(TREE)])
    p_out = [[p_copy(t, at_z(step), p_ssem.at[t, k]) for k, step in enumerate(TREE)] for t in range(2)]

    @pl.when(d == 0)
    def _():
        for copy in p_out[0]:
            copy.start()

    loads[5].wait()

    def left_product(s):
        live = s < count_ref[0, 0]
        left = jnp.dot(p_ref[rows_ref[0, 0, s]], a_buf[s], preferred_element_type=F32)
        left = jnp.where(live, left, 0.0)
        high = left.astype(BF16)
        lhl[s, 0:64] = high
        lhl[s, 64:128] = (left - high.astype(F32)).astype(BF16)

    pl.loop(0, 8)(left_product)

    @pl.when(d == 0)
    def _():
        for copy in p_out[0]:
            copy.wait_send()

    start_when(d == 0, p_out[1])

    pl.loop(8, 16)(left_product)

    for copy in quad_in:
        copy.wait_recv()
    to_smem = pltpu.make_async_copy(agg_quad, quad_s, sm_sem)
    to_smem.start()
    to_smem.wait()
    labels = [quad_s[g // 4, 0, g % 4] for g in range(16)]
    for g in range(16):
        before = jnp.int32(0)
        for o in range(g):
            before = jnp.where(labels[o] == labels[g], o + 1, before)
        rows_s[0, g] = before
    for k, step in enumerate((0,) + FAR):
        wanted = relay_ref[((z + step) % NZ) * 2 + core]
        at = jnp.int32(0)
        for g in range(16):
            at = jnp.where(labels[g] == wanted, g + 1, at)
        rows_s[1, k] = at


    @pl.when(d != 0)
    def _():
        agg_copy(at_z(1), ag_ssem.at[0]).wait_recv()

    pass_on(lambda step, k: agg_copy(at_z(step), af_ssem.at[k]))
    start(remote(agg_col.at[core], agg_col.at[core], as_ssem, as_rsem, sib))

    keys_in = []
    for k in range(1, 4):
        keys_in.append(remote(keys_x.at[0], keys_x.at[k], k_ssem.at[0, k - 1], k_rsem.at[0, k - 1], at_xy(k, 0)))
        keys_in.append(remote(keys_y.at[0], keys_y.at[k], k_ssem.at[1, k - 1], k_rsem.at[1, k - 1], at_xy(0, k)))
    for copy in keys_in:
        pending.append(copy.wait_send)

    def keys_out():
        remote(agg_col.at[1 - core], agg_col.at[1 - core], as_ssem, as_rsem, sib).wait_recv()
        to_smem = pltpu.make_async_copy(agg_col, col_s, sm_sem)
        to_smem.start()
        to_smem.wait()
        for s in range(16):
            j = cols_ref[0, 0, s]
            key = rows_ref[0, 0, s] * 32 + col_s[j // 4, 0, j % 4]
            line = jnp.full((1, 128), jnp.where(s < count_ref[0, 0], key, -1), jnp.int32)
            keys_x[0, s : s + 1] = line
            keys_y[0, s : s + 1] = line
        for copy in keys_in:
            copy.start()

    outside = (d != 0) & jnp.logical_not(in_tree)

    @pl.when(jnp.logical_not(in_tree))
    def _():
        keys_out()

    @pl.when(d != 0)
    def _():
        p_copy(0, at_z(1), p_ssem.at[0, 0]).wait_recv()

    pass_on(lambda step, k: p_copy(0, at_z(step), f_ssem.at[0, k]))
    start(remote(own_half(0), own_half(0), sib_ssem.at[0], sib_rsem.at[0], sib))

    @pl.when(in_tree)
    def _():
        p_copy(1, at_z(1), p_ssem.at[1, 0]).wait_recv()

    pass_on(lambda step, k: p_copy(1, at_z(step), f_ssem.at[1, k]))

    @pl.when(in_tree)
    def _():
        keys_out()

    def sibling_in(t):
        other = p_buf[t].at[1 - core]
        remote(other, other, sib_ssem.at[t], sib_rsem.at[t], sib).wait_recv()

    group = lax.broadcasted_iota(jnp.int32, (64, 128), 1) // 32
    small_group = lax.broadcasted_iota(jnp.int32, (32, 128), 1) // 32
    low = small_group < 2

    def product(t, s, v):
        j = cols_ref[0, 0, s]
        both = jnp.dot(lhl[s], p_buf[t][j // 4], preferred_element_type=F32)
        return pltpu.roll(both[0:64] + both[64:128], ((v + 4 - j % 4) % 4) * 32, 1)

    first_a, first_b = ([], []), ([], [])

    def products_out(t):
        @pl.loop(0, 4)
        def _(u):
            four = product(t, 4 * u, 0)
            for v in range(1, 4):
                four = jnp.where(group == v, product(t, 4 * u + v, v), four)
            g_a[t, 0, u] = four[0:32]
            g_b[t, 0, u] = four[32:64]

        for k in range(1, 4):
            first_a[t].append(start(remote(g_a.at[t, 0], g_a.at[t, k], x_ssem.at[t, 0, k - 1], x_rsem.at[t, 0, k - 1], at_xy(k, 0))))
            first_b[t].append(start(remote(g_b.at[t, 0], g_b.at[t, k], x_ssem.at[t, 1, k - 1], x_rsem.at[t, 1, k - 1], at_xy(0, k))))

    sibling_in(0)
    products_out(0)

    @pl.when(outside)
    def _():
        p_copy(1, at_z(1), p_ssem.at[1, 0]).wait_recv()

    start(remote(own_half(1), own_half(1), sib_ssem.at[1], sib_rsem.at[1], sib))

    for copy in keys_in:
        copy.wait_recv()
    lane_i = lax.broadcasted_iota(jnp.int32, (64, 128), 1)
    slot_i = lax.broadcasted_iota(jnp.int32, (64, 128), 0)
    table[...] = jnp.zeros((8, 128), jnp.int32)
    for h, keys in enumerate((keys_x, keys_y)):
        down = keys[...].reshape(64, 128)
        across = jnp.sum(jnp.where(slot_i == lane_i, down, 0), axis=0, keepdims=True)
        before = jnp.where((down == across) & (slot_i < lane_i), slot_i + 1, 0)
        table[2 * h : 2 * h + 1] = jnp.max(before, axis=0, keepdims=True)
        table[2 * h + 1 : 2 * h + 2] = jnp.max(jnp.where(down == lane_i, slot_i + 1, 0), axis=0, keepdims=True)
    to_smem = pltpu.make_async_copy(table, table_s, sm_sem)
    to_smem.start()

    sibling_in(1)
    products_out(1)
    to_smem.wait()

    run_a[0] = jnp.zeros((32, 128), F32)
    run_b[0] = jnp.zeros((32, 128), F32)
    second_a, second_b = ([], []), ([], [])

    def join(parts):
        left = jnp.where(small_group == 0, parts[0], parts[1])
        return jnp.where(low, left, jnp.where(small_group == 2, parts[2], parts[3]))

    def blocks(run, h, first_key):
        return join([run[table_s[2 * h + 1, first_key + o]] for o in (0, 1, 32, 33)])

    def sums_out(t):
        for k in range(4):
            if k:
                first_a[t][k - 1].wait_recv()
                first_b[t][k - 1].wait_recv()

            @pl.loop(0, 4)
            def _(u):
                for h, (got, run) in enumerate(((g_a, run_a), (g_b, run_b))):
                    turned = [got[t, k, u]]
                    for o in range(1, 4):
                        turned.append(pltpu.roll(turned[0], 32 * o, 1))
                    for v in range(4):
                        s = k * 16 + 4 * u + v
                        parts = [turned[(g + 4 - v) % 4] for g in range(4)]
                        run[s + 1] = join(parts) + run[table_s[2 * h, s]]

        for k in (1, 2, 3, 0):
            there = ((y + k) % NY) * NX + x
            for n in range(2):
                e_a[t, k, n] = blocks(run_a, 0, n * 64 + there * 2)
            if k:
                second_a[t].append(start(remote(e_a.at[t, k], r2_a.at[t, k - 1], x2_ssem.at[t, 0, k - 1], x2_rsem.at[t, 0, k - 1], at_xy(0, k))))
            there = y * NX + (x + k) % NX
            for n in range(2):
                e_b[t, k, n] = blocks(run_b, 1, n * 64 + there * 2)
            if k:
                second_b[t].append(start(remote(e_b.at[t, k], r2_b.at[t, k - 1], x2_ssem.at[t, 1, k - 1], x2_rsem.at[t, 1, k - 1], at_xy(k, 0))))

    sums_out(0)
    sums_out(1)

    to_pair, to_sib, on_sib = [], [], []
    for h in range(2):
        for copy in second_a[h] + second_b[h]:
            copy.wait_recv()
        for n in range(2):
            top = (e_a[h, 0, n] + r2_a[h, 0, n]) + (r2_a[h, 1, n] + r2_a[h, 2, n])
            bottom = (e_b[h, 0, n] + r2_b[h, 0, n]) + (r2_b[h, 1, n] + r2_b[h, 2, n])
            quad[0, h, 2 * n] = jnp.where(low, top, pltpu.roll(bottom, 64, 1))
            quad[0, h, 2 * n + 1] = jnp.where(low, pltpu.roll(top, 64, 1), bottom)
        to_pair.append(start(remote(quad.at[0, h], quad.at[2, h], z_ssem.at[h, 1], z_rsem.at[h, 1], quad_same)))
        to_sib.append(start(remote(quad.at[0, h], quad.at[1, h], z_ssem.at[h, 0], z_rsem.at[h, 0], sib)))
        on_sib.append(remote(quad.at[2, h], quad.at[3, h], z_ssem.at[h, 2], z_rsem.at[h, 2], sib))

    def chain(h, group):
        for g in range(group * 4, group * 4 + 4):
            run_z[h, g + 1] = quad[group, h, g % 4] + run_z[h, rows_s[0, g]]

    far, far_scale = ([], []), ([], [])
    diagonal = lax.broadcasted_iota(jnp.int32, (32, 128), 0) == lax.broadcasted_iota(jnp.int32, (32, 128), 1)
    for h in range(2):
        run_z[h, 0] = jnp.zeros((32, 128), F32)
        chain(h, 0)
        to_sib[h].wait_recv()
        chain(h, 1)
        to_pair[h].wait_recv()
        start(on_sib[h])
        chain(h, 2)
        on_sib[h].wait_recv()
        chain(h, 3)
        own[h] = run_z[h, rows_s[1, 0]]
        for k, step in enumerate(FAR):
            block = run_z[h, rows_s[1, k + 1]]
            largest = jnp.maximum(jnp.max(jnp.abs(block), axis=1, keepdims=True), 1e-30)
            ob[h, k] = jnp.round(block * (STEPS / largest)).astype(jnp.int32).astype(jnp.int16)
            scale[h, k] = jnp.sum(jnp.where(diagonal, largest, 0.0), axis=0, keepdims=True)
            far[h].append(start(remote(ob.at[h, k], rz.at[h, k], w_ssem.at[h, k], w_rsem.at[h, k], at_z(step))))
            far_scale[h].append(start(remote(scale.at[h, k], scale_in.at[h, k], v_ssem.at[h, k], v_rsem.at[h, k], at_z(step))))

    spread = ([], [])
    for h in range(2):
        total = own[h]
        for k in range(len(FAR)):
            far_scale[h][k].wait_recv()
            largest = jnp.sum(jnp.where(diagonal, scale_in[h, k], 0.0), axis=1, keepdims=True)
            far[h][k].wait_recv()
            total = total + rz[h, k].astype(jnp.int32).astype(F32) * (largest / STEPS)
        tile[h] = total
        for k, (dx, dy) in enumerate(plane):
            spread[h].append(start(remote(tile.at[h], gat.at[h, k], o_ssem.at[h, k], o_rsem.at[h, k], at_xy(dx, dy))))

    def place(source, first, second):
        there = pl.ds(pl.multiple_of(source * 128, 128), 128)
        out_ref[0, 0:32, there] = jnp.where(
            low,
            jnp.where(small_group == 0, first, pltpu.roll(second, 32, 1)),
            jnp.where(small_group == 2, pltpu.roll(first, 32, 1), pltpu.roll(second, 64, 1)),
        )
        out_ref[0, 32:64, there] = jnp.where(
            low,
            jnp.where(small_group == 0, pltpu.roll(first, 64, 1), pltpu.roll(second, 96, 1)),
            jnp.where(small_group == 2, pltpu.roll(first, 96, 1), second),
        )

    place(col, tile[0], tile[1])
    for copy in spread[0]:
        copy.wait_recv()
    for k, (dx, dy) in enumerate(plane):
        spread[1][k].wait_recv()
        source = ((y + NY - dy) % NY) * NX + (x + NX - dx) % NX
        place(source, gat[0, k], gat[1, k])
    finish()


def on_device(a_blocks, slot_row, slot_col, slot_count, p_blocks, aggregate, relayout):
    hbm = pl.BlockSpec(memory_space=pltpu.HBM)
    vmem = pl.BlockSpec(memory_space=pltpu.VMEM)
    dma = pltpu.SemaphoreType.DMA
    return pl.pallas_call(
        kernel,
        out_shape=pltpu.VMEM((1, 64, 2048), F32),
        in_specs=[hbm, hbm, hbm, hbm, vmem, hbm, hbm],
        out_specs=vmem,
        scratch_shapes=[
            pltpu.VMEM((16, 320, 320), BF16),
            pltpu.VMEM((16, 128, 320), BF16),
            pltpu.VMEM((2, 320, 128), BF16),
            pltpu.VMEM((2, 320, 128), BF16),
            pltpu.SMEM((1, 1, 16), jnp.int32),
            pltpu.SMEM((1, 1, 16), jnp.int32),
            pltpu.SMEM((1, 1), jnp.int32),
            pltpu.SMEM((4,), jnp.int32),
            pltpu.SMEM((32,), jnp.int32),
            pltpu.VMEM((8, 128), jnp.int32),
            pltpu.VMEM((2, 8, 128), jnp.int32),
            pltpu.VMEM((4, 8, 128), jnp.int32),
            pltpu.VMEM((4, 16, 128), jnp.int32),
            pltpu.VMEM((4, 16, 128), jnp.int32),
            pltpu.VMEM((8, 128), jnp.int32),
            pltpu.SMEM((2, 8, 128), jnp.int32),
            pltpu.SMEM((4, 8, 128), jnp.int32),
            pltpu.SMEM((8, 128), jnp.int32),
            pltpu.SMEM((2, 16), jnp.int32),
            pltpu.VMEM((2, 4, 4, 32, 128), F32),
            pltpu.VMEM((2, 4, 4, 32, 128), F32),
            pltpu.VMEM((65, 32, 128), F32),
            pltpu.VMEM((65, 32, 128), F32),
            pltpu.VMEM((2, 4, 2, 32, 128), F32),
            pltpu.VMEM((2, 4, 2, 32, 128), F32),
            pltpu.VMEM((2, 3, 2, 32, 128), F32),
            pltpu.VMEM((2, 3, 2, 32, 128), F32),
            pltpu.VMEM((4, 2, 4, 32, 128), F32),
            pltpu.VMEM((2, 17, 32, 128), F32),
            pltpu.VMEM((2, 32, 128), F32),
            pltpu.VMEM((2, 7, 32, 128), jnp.int16),
            pltpu.VMEM((2, 7, 32, 128), jnp.int16),
            pltpu.VMEM((2, 7, 1, 128), F32),
            pltpu.VMEM((2, 7, 1, 128), F32),
            pltpu.VMEM((2, 32, 128), F32),
            pltpu.VMEM((2, 15, 32, 128), F32),
            dma((6,)), dma,
            dma((2, 4)), dma((2,)), dma((2, 4)), dma((2,)), dma((2,)),
            dma((4,)), dma, dma((4,)), dma, dma,
            dma((3,)), dma((3,)), dma((2, 3)), dma((2, 3)),
            dma((2, 2, 3)), dma((2, 2, 3)), dma((2, 2, 3)), dma((2, 2, 3)),
            dma((2, 3)), dma((2, 3)), dma((2, 7)), dma((2, 7)), dma((2, 7)), dma((2, 7)), dma((2, 15)), dma((2, 15)),
        ],
        compiler_params=pltpu.CompilerParams(
            collective_id=0, has_side_effects=True, vmem_limit_bytes=60 << 20
        ),
        name="coarse_operator",
    )(a_blocks, slot_row, slot_col, slot_count, jnp.swapaxes(p_blocks, 1, 2), aggregate, relayout)


def solution(mesh):
    return jax.shard_map(
        on_device,
        mesh=mesh,
        in_specs=(
            P("row", "col", None, None, None),
            P("row", "col", None),
            P("row", "col", None),
            P("row", "col"),
            P("row", None, None),
            P("row"),
            P(),
        ),
        out_specs=P("row", None, None),
        check_vma=False,
    )
```

```python
import functools

import jax
import jax.numpy as jnp
from jax import lax
from jax.experimental import pallas as pl
from jax.experimental.pallas import tpu as pltpu
from jax.sharding import PartitionSpec as P

MESH = pl.DeviceIdType.MESH

NX, NY, NZ = 4, 4, 16
TREE = (6, 10, 2, 14)
FAR = (8, 6, 10, 4, 12, 2, 14)
RING = (6, 10, 4, 12, 2, 14, 1, 15)
STEPS = 32767.0
F32 = jnp.float32
BF16 = jnp.bfloat16


def kernel(
    a_hbm, rows_hbm, cols_hbm, count_hbm, p_ref, agg_hbm, relay_hbm, out_ref,
    a_buf, lhl, p_buf0, p_buf1, rows_ref, cols_ref, count_ref, agg_ref, relay_ref,
    agg_mine, agg_col, agg_quad, keys_x, keys_y, table, col_s, quad_s, table_s, rows_s,
    g_a, g_b, run_a, run_b, e_a, e_b, r2_a, r2_b, quad, run_z, own, ob, rz, scale, scale_in, tile, gat,
    heard, loc_sem, sm_sem, p_ssem, p_rsem, f_ssem, sib_ssem, sib_rsem, ag_ssem, ag_rsem, af_ssem, as_ssem, as_rsem,
    q_ssem, q_rsem, k_ssem, k_rsem, x_ssem, x_rsem, x2_ssem, x2_rsem, z_ssem, z_rsem, w_ssem, w_rsem, v_ssem, v_rsem, o_ssem, o_rsem,
):
    row = lax.axis_index("row")
    col = lax.axis_index("col")
    z, core = row // 2, row % 2
    y, x = col // NX, col % NX
    sib = (z * 2 + 1 - core, col)
    zpair = z + 1 - 2 * (z % 2)
    quad_same = (zpair * 2 + core, col)
    quad_diag = (zpair * 2 + 1 - core, col)
    pending = []
    p_buf = (p_buf0, p_buf1)

    def at_z(step):
        return (((z + step) % NZ) * 2 + core, col)

    def at_xy(dx, dy):
        return (row, ((y + dy) % NY) * NX + (x + dx) % NX)

    def remote(src, dst, ssem, rsem, dev):
        return pltpu.make_async_remote_copy(
            src_ref=src, dst_ref=dst, send_sem=ssem, recv_sem=rsem, device_id=dev, device_id_type=MESH
        )

    def start(copy):
        copy.start()
        pending.append(copy.wait_send)
        return copy

    def finish():
        for wait in pending:
            wait()

    barrier = pltpu.get_barrier_semaphore()
    plane = sorted(((o % NX, o // NX) for o in range(1, NX * NY)), key=lambda o: -min(o[0], NX - o[0]) - min(o[1], NY - o[1]))
    partners = [at_z(step) for step in RING] + [at_xy(dx, dy) for dx, dy in plane] + [sib, quad_diag]
    for dev in partners:
        pl.semaphore_signal(barrier, inc=1, device_id=dev, device_id_type=MESH)

    small = ((rows_hbm, rows_ref), (cols_hbm, cols_ref), (count_hbm, count_ref), (agg_hbm, agg_ref), (relay_hbm, relay_ref))
    loads = [pltpu.make_async_copy(src, dst, loc_sem.at[k]) for k, (src, dst) in enumerate(small)]
    loads.append(pltpu.make_async_copy(a_hbm.at[0, 0], a_buf, loc_sem.at[5]))
    for load in loads:
        load.start()
    for load in loads[:5]:
        load.wait()

    lane8 = lax.broadcasted_iota(jnp.int32, (8, 128), 1)
    mine = jnp.zeros((8, 128), jnp.int32)
    for i in range(4):
        mine = jnp.where(lane8 == i, agg_ref[i], mine)
    agg_mine[...] = mine
    agg_quad[0] = mine
    d = (z + NZ - col) % NZ

    @pl.when(d == 0)
    def _():
        agg_col[core] = mine
        for t in range(2):
            both = jnp.concatenate([p_ref[i, 32 * t : 32 * t + 32] for i in range(4)], axis=0)
            p_buf[t][core] = both.astype(F32).T.astype(BF16)

    pl.semaphore_wait(barrier, len(partners))

    for step in (2, 14):
        pl.semaphore_signal(heard, inc=1, device_id=at_z(step), device_id_type=MESH)

    in_tree = d == TREE[0]
    for step in TREE[1:]:
        in_tree = in_tree | (d == step)

    def own_half(t):
        return p_buf[t].at[core]

    def agg_copy(dev, ssem):
        return remote(agg_col.at[core], agg_col.at[core], ssem, ag_rsem, dev)

    def p_copy(t, dev, ssem):
        return remote(own_half(t), own_half(t), ssem, p_rsem.at[t], dev)

    def start_when(condition, copies):
        @pl.when(condition)
        def _():
            for copy in copies:
                copy.start()

        def wait():
            @pl.when(condition)
            def _():
                for copy in copies:
                    copy.wait_send()

        pending.append(wait)

    def pass_on(copy_to):
        start_when((d == 6) | (d == 10), [copy_to(2, 0)])
        start_when(d == 6, [copy_to(14, 1)])
        start_when(in_tree, [copy_to(1, 2), copy_to(15, 3)])

    quad_devs = (sib, quad_same, quad_diag)
    start_when(d == 0, [agg_copy(at_z(step), ag_ssem.at[k]) for k, step in enumerate(TREE)])
    p_out = [[p_copy(t, at_z(step), p_ssem.at[t, k]) for k, step in enumerate(TREE)] for t in range(2)]

    @pl.when(d == 0)
    def _():
        for copy in p_out[0]:
            copy.start()

    quad_in = [start(remote(agg_mine, agg_quad.at[k + 1], q_ssem.at[k], q_rsem.at[k], quad_devs[k])) for k in range(3)]

    loads[5].wait()

    def left_product(s):
        live = s < count_ref[0, 0]
        left = jnp.dot(p_ref[rows_ref[0, 0, s]], a_buf[s], preferred_element_type=F32)
        left = jnp.where(live, left, 0.0)
        high = left.astype(BF16)
        lhl[s, 0:64] = high
        lhl[s, 64:128] = (left - high.astype(F32)).astype(BF16)

    pl.loop(0, 8)(left_product)

    @pl.when(d == 0)
    def _():
        for copy in p_out[0]:
            copy.wait_send()

    start_when(d == 0, p_out[1])

    pl.loop(8, 16)(left_product)

    for copy in quad_in:
        copy.wait_recv()
    to_smem = pltpu.make_async_copy(agg_quad, quad_s, sm_sem)
    to_smem.start()
    to_smem.wait()
    labels = [quad_s[g // 4, 0, g % 4] for g in range(16)]
    for g in range(16):
        before = jnp.int32(0)
        for o in range(g):
            before = jnp.where(labels[o] == labels[g], o + 1, before)
        rows_s[0, g] = before
    for k, step in enumerate((0,) + FAR):
        wanted = relay_ref[((z + step) % NZ) * 2 + core]
        at = jnp.int32(0)
        for g in range(16):
            at = jnp.where(labels[g] == wanted, g + 1, at)
        rows_s[1, k] = at


    @pl.when(d != 0)
    def _():
        agg_copy(at_z(1), ag_ssem.at[0]).wait_recv()

    pass_on(lambda step, k: agg_copy(at_z(step), af_ssem.at[k]))
    start(remote(agg_col.at[core], agg_col.at[core], as_ssem, as_rsem, sib))

    keys_in = []
    for k in range(1, 4):
        keys_in.append(remote(keys_x.at[0], keys_x.at[k], k_ssem.at[0, k - 1], k_rsem.at[0, k - 1], at_xy(k, 0)))
        keys_in.append(remote(keys_y.at[0], keys_y.at[k], k_ssem.at[1, k - 1], k_rsem.at[1, k - 1], at_xy(0, k)))
    for copy in keys_in:
        pending.append(copy.wait_send)

    def keys_out():
        remote(agg_col.at[1 - core], agg_col.at[1 - core], as_ssem, as_rsem, sib).wait_recv()
        to_smem = pltpu.make_async_copy(agg_col, col_s, sm_sem)
        to_smem.start()
        to_smem.wait()
        for s in range(16):
            j = cols_ref[0, 0, s]
            key = rows_ref[0, 0, s] * 32 + col_s[j // 4, 0, j % 4]
            line = jnp.full((1, 128), jnp.where(s < count_ref[0, 0], key, -1), jnp.int32)
            keys_x[0, s : s + 1] = line
            keys_y[0, s : s + 1] = line
        for copy in keys_in:
            copy.start()

    outside = (d != 0) & jnp.logical_not(in_tree)

    @pl.when(jnp.logical_not(in_tree))
    def _():
        keys_out()

    @pl.when(d != 0)
    def _():
        p_copy(0, at_z(1), p_ssem.at[0, 0]).wait_recv()

    pass_on(lambda step, k: p_copy(0, at_z(step), f_ssem.at[0, k]))
    start(remote(own_half(0), own_half(0), sib_ssem.at[0], sib_rsem.at[0], sib))

    @pl.when(in_tree)
    def _():
        p_copy(1, at_z(1), p_ssem.at[1, 0]).wait_recv()

    pass_on(lambda step, k: p_copy(1, at_z(step), f_ssem.at[1, k]))

    @pl.when(in_tree)
    def _():
        keys_out()

    def sibling_in(t):
        other = p_buf[t].at[1 - core]
        remote(other, other, sib_ssem.at[t], sib_rsem.at[t], sib).wait_recv()

    group = lax.broadcasted_iota(jnp.int32, (64, 128), 1) // 32
    small_group = lax.broadcasted_iota(jnp.int32, (32, 128), 1) // 32
    low = small_group < 2

    def product(t, s, v):
        j = cols_ref[0, 0, s]
        both = jnp.dot(lhl[s], p_buf[t][j // 4], preferred_element_type=F32)
        return pltpu.roll(both[0:64] + both[64:128], ((v + 4 - j % 4) % 4) * 32, 1)

    first_a, first_b = ([], []), ([], [])

    def products_out(t):
        @pl.loop(0, 4)
        def _(u):
            four = product(t, 4 * u, 0)
            for v in range(1, 4):
                four = jnp.where(group == v, product(t, 4 * u + v, v), four)
            g_a[t, 0, u] = four[0:32]
            g_b[t, 0, u] = four[32:64]

        for k in range(1, 4):
            first_a[t].append(start(remote(g_a.at[t, 0], g_a.at[t, k], x_ssem.at[t, 0, k - 1], x_rsem.at[t, 0, k - 1], at_xy(k, 0))))
            first_b[t].append(start(remote(g_b.at[t, 0], g_b.at[t, k], x_ssem.at[t, 1, k - 1], x_rsem.at[t, 1, k - 1], at_xy(0, k))))

    sibling_in(0)
    products_out(0)

    @pl.when(outside)
    def _():
        p_copy(1, at_z(1), p_ssem.at[1, 0]).wait_recv()

    start(remote(own_half(1), own_half(1), sib_ssem.at[1], sib_rsem.at[1], sib))

    for copy in keys_in:
        copy.wait_recv()
    lane_i = lax.broadcasted_iota(jnp.int32, (64, 128), 1)
    slot_i = lax.broadcasted_iota(jnp.int32, (64, 128), 0)
    table[...] = jnp.zeros((8, 128), jnp.int32)
    for h, keys in enumerate((keys_x, keys_y)):
        down = keys[...].reshape(64, 128)
        across = jnp.sum(jnp.where(slot_i == lane_i, down, 0), axis=0, keepdims=True)
        before = jnp.where((down == across) & (slot_i < lane_i), slot_i + 1, 0)
        table[2 * h : 2 * h + 1] = jnp.max(before, axis=0, keepdims=True)
        table[2 * h + 1 : 2 * h + 2] = jnp.max(jnp.where(down == lane_i, slot_i + 1, 0), axis=0, keepdims=True)
    to_smem = pltpu.make_async_copy(table, table_s, sm_sem)
    to_smem.start()

    sibling_in(1)
    products_out(1)
    to_smem.wait()

    run_a[0] = jnp.zeros((32, 128), F32)
    run_b[0] = jnp.zeros((32, 128), F32)
    second_a, second_b = ([], []), ([], [])

    def join(parts):
        left = jnp.where(small_group == 0, parts[0], parts[1])
        return jnp.where(low, left, jnp.where(small_group == 2, parts[2], parts[3]))

    def blocks(run, h, first_key):
        return join([run[table_s[2 * h + 1, first_key + o]] for o in (0, 1, 32, 33)])

    def sums_out(t):
        for k in range(4):
            if k:
                first_a[t][k - 1].wait_recv()
                first_b[t][k - 1].wait_recv()

            @pl.loop(0, 4)
            def _(u):
                for h, (got, run) in enumerate(((g_a, run_a), (g_b, run_b))):
                    turned = [got[t, k, u]]
                    for o in range(1, 4):
                        turned.append(pltpu.roll(turned[0], 32 * o, 1))
                    for v in range(4):
                        s = k * 16 + 4 * u + v
                        parts = [turned[(g + 4 - v) % 4] for g in range(4)]
                        run[s + 1] = join(parts) + run[table_s[2 * h, s]]

        for k in (1, 2, 3, 0):
            there = ((y + k) % NY) * NX + x
            for n in range(2):
                e_a[t, k, n] = blocks(run_a, 0, n * 64 + there * 2)
            if k:
                second_a[t].append(start(remote(e_a.at[t, k], r2_a.at[t, k - 1], x2_ssem.at[t, 0, k - 1], x2_rsem.at[t, 0, k - 1], at_xy(0, k))))
            there = y * NX + (x + k) % NX
            for n in range(2):
                e_b[t, k, n] = blocks(run_b, 1, n * 64 + there * 2)
            if k:
                second_b[t].append(start(remote(e_b.at[t, k], r2_b.at[t, k - 1], x2_ssem.at[t, 1, k - 1], x2_rsem.at[t, 1, k - 1], at_xy(k, 0))))

    sums_out(0)
    sums_out(1)

    to_pair, to_sib, on_sib = [], [], []
    for h in range(2):
        for copy in second_a[h] + second_b[h]:
            copy.wait_recv()
        for n in range(2):
            top = (e_a[h, 0, n] + r2_a[h, 0, n]) + (r2_a[h, 1, n] + r2_a[h, 2, n])
            bottom = (e_b[h, 0, n] + r2_b[h, 0, n]) + (r2_b[h, 1, n] + r2_b[h, 2, n])
            quad[0, h, 2 * n] = jnp.where(low, top, pltpu.roll(bottom, 64, 1))
            quad[0, h, 2 * n + 1] = jnp.where(low, pltpu.roll(top, 64, 1), bottom)
        to_pair.append(start(remote(quad.at[0, h], quad.at[2, h], z_ssem.at[h, 1], z_rsem.at[h, 1], quad_same)))
        to_sib.append(start(remote(quad.at[0, h], quad.at[1, h], z_ssem.at[h, 0], z_rsem.at[h, 0], sib)))
        on_sib.append(remote(quad.at[2, h], quad.at[3, h], z_ssem.at[h, 2], z_rsem.at[h, 2], sib))

    def chain(h, group):
        for g in range(group * 4, group * 4 + 4):
            run_z[h, g + 1] = quad[group, h, g % 4] + run_z[h, rows_s[0, g]]

    pl.semaphore_wait(heard, 2)

    far, far_scale = ([], []), ([], [])
    diagonal = lax.broadcasted_iota(jnp.int32, (32, 128), 0) == lax.broadcasted_iota(jnp.int32, (32, 128), 1)
    for h in range(2):
        run_z[h, 0] = jnp.zeros((32, 128), F32)
        chain(h, 0)
        to_sib[h].wait_recv()
        chain(h, 1)
        to_pair[h].wait_recv()
        start(on_sib[h])
        chain(h, 2)
        on_sib[h].wait_recv()
        chain(h, 3)
        own[h] = run_z[h, rows_s[1, 0]]
        for k, step in enumerate(FAR):
            block = run_z[h, rows_s[1, k + 1]]
            largest = jnp.maximum(jnp.max(jnp.abs(block), axis=1, keepdims=True), 1e-30)
            ob[h, k] = jnp.round(block * (STEPS / largest)).astype(jnp.int32).astype(jnp.int16)
            scale[h, k] = jnp.sum(jnp.where(diagonal, largest, 0.0), axis=0, keepdims=True)
            far[h].append(start(remote(ob.at[h, k], rz.at[h, k], w_ssem.at[h, k], w_rsem.at[h, k], at_z(step))))
            far_scale[h].append(start(remote(scale.at[h, k], scale_in.at[h, k], v_ssem.at[h, k], v_rsem.at[h, k], at_z(step))))

    spread = ([], [])
    for h in range(2):
        total = own[h]
        for k in range(len(FAR)):
            far_scale[h][k].wait_recv()
            largest = jnp.sum(jnp.where(diagonal, scale_in[h, k], 0.0), axis=1, keepdims=True)
            far[h][k].wait_recv()
            total = total + rz[h, k].astype(jnp.int32).astype(F32) * (largest / STEPS)
        tile[h] = total
        for k, (dx, dy) in enumerate(plane):
            spread[h].append(start(remote(tile.at[h], gat.at[h, k], o_ssem.at[h, k], o_rsem.at[h, k], at_xy(dx, dy))))

    def place(source, first, second):
        there = pl.ds(pl.multiple_of(source * 128, 128), 128)
        out_ref[0, 0:32, there] = jnp.where(
            low,
            jnp.where(small_group == 0, first, pltpu.roll(second, 32, 1)),
            jnp.where(small_group == 2, pltpu.roll(first, 32, 1), pltpu.roll(second, 64, 1)),
        )
        out_ref[0, 32:64, there] = jnp.where(
            low,
            jnp.where(small_group == 0, pltpu.roll(first, 64, 1), pltpu.roll(second, 96, 1)),
            jnp.where(small_group == 2, pltpu.roll(first, 96, 1), second),
        )

    place(col, tile[0], tile[1])
    for copy in spread[0]:
        copy.wait_recv()
    for k, (dx, dy) in enumerate(plane):
        spread[1][k].wait_recv()
        source = ((y + NY - dy) % NY) * NX + (x + NX - dx) % NX
        place(source, gat[0, k], gat[1, k])
    finish()


def on_device(a_blocks, slot_row, slot_col, slot_count, p_blocks, aggregate, relayout):
    hbm = pl.BlockSpec(memory_space=pltpu.HBM)
    vmem = pl.BlockSpec(memory_space=pltpu.VMEM)
    dma = pltpu.SemaphoreType.DMA
    return pl.pallas_call(
        kernel,
        out_shape=pltpu.VMEM((1, 64, 2048), F32),
        in_specs=[hbm, hbm, hbm, hbm, vmem, hbm, hbm],
        out_specs=vmem,
        scratch_shapes=[
            pltpu.VMEM((16, 320, 320), BF16),
            pltpu.VMEM((16, 128, 320), BF16),
            pltpu.VMEM((2, 320, 128), BF16),
            pltpu.VMEM((2, 320, 128), BF16),
            pltpu.SMEM((1, 1, 16), jnp.int32),
            pltpu.SMEM((1, 1, 16), jnp.int32),
            pltpu.SMEM((1, 1), jnp.int32),
            pltpu.SMEM((4,), jnp.int32),
            pltpu.SMEM((32,), jnp.int32),
            pltpu.VMEM((8, 128), jnp.int32),
            pltpu.VMEM((2, 8, 128), jnp.int32),
            pltpu.VMEM((4, 8, 128), jnp.int32),
            pltpu.VMEM((4, 16, 128), jnp.int32),
            pltpu.VMEM((4, 16, 128), jnp.int32),
            pltpu.VMEM((8, 128), jnp.int32),
            pltpu.SMEM((2, 8, 128), jnp.int32),
            pltpu.SMEM((4, 8, 128), jnp.int32),
            pltpu.SMEM((8, 128), jnp.int32),
            pltpu.SMEM((2, 16), jnp.int32),
            pltpu.VMEM((2, 4, 4, 32, 128), F32),
            pltpu.VMEM((2, 4, 4, 32, 128), F32),
            pltpu.VMEM((65, 32, 128), F32),
            pltpu.VMEM((65, 32, 128), F32),
            pltpu.VMEM((2, 4, 2, 32, 128), F32),
            pltpu.VMEM((2, 4, 2, 32, 128), F32),
            pltpu.VMEM((2, 3, 2, 32, 128), F32),
            pltpu.VMEM((2, 3, 2, 32, 128), F32),
            pltpu.VMEM((4, 2, 4, 32, 128), F32),
            pltpu.VMEM((2, 17, 32, 128), F32),
            pltpu.VMEM((2, 32, 128), F32),
            pltpu.VMEM((2, 7, 32, 128), jnp.int16),
            pltpu.VMEM((2, 7, 32, 128), jnp.int16),
            pltpu.VMEM((2, 7, 1, 128), F32),
            pltpu.VMEM((2, 7, 1, 128), F32),
            pltpu.VMEM((2, 32, 128), F32),
            pltpu.VMEM((2, 15, 32, 128), F32),
            pltpu.SemaphoreType.REGULAR, dma((6,)), dma,
            dma((2, 4)), dma((2,)), dma((2, 4)), dma((2,)), dma((2,)),
            dma((4,)), dma, dma((4,)), dma, dma,
            dma((3,)), dma((3,)), dma((2, 3)), dma((2, 3)),
            dma((2, 2, 3)), dma((2, 2, 3)), dma((2, 2, 3)), dma((2, 2, 3)),
            dma((2, 3)), dma((2, 3)), dma((2, 7)), dma((2, 7)), dma((2, 7)), dma((2, 7)), dma((2, 15)), dma((2, 15)),
        ],
        compiler_params=pltpu.CompilerParams(
            collective_id=0, has_side_effects=True, vmem_limit_bytes=60 << 20
        ),
        name="coarse_operator",
    )(a_blocks, slot_row, slot_col, slot_count, jnp.swapaxes(p_blocks, 1, 2), aggregate, relayout)


def solution(mesh):
    return jax.shard_map(
        on_device,
        mesh=mesh,
        in_specs=(
            P("row", "col", None, None, None),
            P("row", "col", None),
            P("row", "col", None),
            P("row", "col"),
            P("row", None, None),
            P("row"),
            P(),
        ),
        out_specs=P("row", None, None),
        check_vma=False,
    )
```

```python
import functools

import jax
import jax.numpy as jnp
from jax import lax
from jax.experimental import pallas as pl
from jax.experimental.pallas import tpu as pltpu
from jax.sharding import PartitionSpec as P

MESH = pl.DeviceIdType.MESH

NX, NY, NZ = 4, 4, 16
TREE = (6, 10, 2, 14)
FAR = (8, 6, 10, 4, 12, 2, 14)
RING = (8, 6, 10, 4, 12, 2, 14, 1, 15)
STEPS = 32767.0
F32 = jnp.float32
BF16 = jnp.bfloat16


def kernel(
    a_hbm, rows_hbm, cols_hbm, count_hbm, p_ref, agg_hbm, relay_hbm, out_ref,
    a_buf, lhl, p_buf0, p_buf1, rows_ref, cols_ref, count_ref, agg_ref, relay_ref,
    agg_mine, agg_col, agg_quad, keys_x, keys_y, table, col_s, quad_s, table_s, rows_s,
    g_a, g_b, run_a, run_b, e_a, e_b, r2_a, r2_b, quad, run_z, own, ob, rz, scale, scale_in, tile, gat,
    loc_sem, sm_sem, p_ssem, p_rsem, f_ssem, sib_ssem, sib_rsem, ag_ssem, ag_rsem, af_ssem, as_ssem, as_rsem,
    q_ssem, q_rsem, k_ssem, k_rsem, x_ssem, x_rsem, x2_ssem, x2_rsem, z_ssem, z_rsem, w_ssem, w_rsem, v_ssem, v_rsem, o_ssem, o_rsem,
):
    row = lax.axis_index("row")
    col = lax.axis_index("col")
    z, core = row // 2, row % 2
    y, x = col // NX, col % NX
    sib = (z * 2 + 1 - core, col)
    zpair = z + 1 - 2 * (z % 2)
    quad_same = (zpair * 2 + core, col)
    quad_diag = (zpair * 2 + 1 - core, col)
    pending = []
    p_buf = (p_buf0, p_buf1)

    def at_z(step):
        return (((z + step) % NZ) * 2 + core, col)

    def at_xy(dx, dy):
        return (row, ((y + dy) % NY) * NX + (x + dx) % NX)

    def remote(src, dst, ssem, rsem, dev):
        return pltpu.make_async_remote_copy(
            src_ref=src, dst_ref=dst, send_sem=ssem, recv_sem=rsem, device_id=dev, device_id_type=MESH
        )

    def start(copy):
        copy.start()
        pending.append(copy.wait_send)
        return copy

    def finish():
        for wait in pending:
            wait()

    barrier = pltpu.get_barrier_semaphore()
    plane = sorted(((o % NX, o // NX) for o in range(1, NX * NY)), key=lambda o: -min(o[0], NX - o[0]) - min(o[1], NY - o[1]))
    partners = [at_z(step) for step in RING] + [at_xy(dx, dy) for dx, dy in plane] + [sib, quad_diag]
    for dev in partners:
        pl.semaphore_signal(barrier, inc=1, device_id=dev, device_id_type=MESH)

    small = ((rows_hbm, rows_ref), (cols_hbm, cols_ref), (count_hbm, count_ref), (agg_hbm, agg_ref), (relay_hbm, relay_ref))
    loads = [pltpu.make_async_copy(src, dst, loc_sem.at[k]) for k, (src, dst) in enumerate(small)]
    loads.append(pltpu.make_async_copy(a_hbm.at[0, 0], a_buf, loc_sem.at[5]))
    for load in loads:
        load.start()
    for load in loads[:5]:
        load.wait()

    lane8 = lax.broadcasted_iota(jnp.int32, (8, 128), 1)
    mine = jnp.zeros((8, 128), jnp.int32)
    for i in range(4):
        mine = jnp.where(lane8 == i, agg_ref[i], mine)
    agg_mine[...] = mine
    agg_quad[0] = mine
    d = (z + NZ - col) % NZ

    @pl.when(d == 0)
    def _():
        agg_col[core] = mine
        for t in range(2):
            both = jnp.concatenate([p_ref[i, 32 * t : 32 * t + 32] for i in range(4)], axis=0)
            p_buf[t][core] = both.astype(F32).T.astype(BF16)

    pl.semaphore_wait(barrier, len(partners))

    in_tree = d == TREE[0]
    for step in TREE[1:]:
        in_tree = in_tree | (d == step)

    def own_half(t):
        return p_buf[t].at[core]

    def agg_copy(dev, ssem):
        return remote(agg_col.at[core], agg_col.at[core], ssem, ag_rsem, dev)

    def p_copy(t, dev, ssem):
        return remote(own_half(t), own_half(t), ssem, p_rsem.at[t], dev)

    def start_when(condition, copies):
        @pl.when(condition)
        def _():
            for copy in copies:
                copy.start()

        def wait():
            @pl.when(condition)
            def _():
                for copy in copies:
                    copy.wait_send()

        pending.append(wait)

    def pass_on(copy_to):
        start_when((d == 6) | (d == 10), [copy_to(2, 0)])
        start_when(d == 6, [copy_to(14, 1)])
        start_when(in_tree, [copy_to(1, 2), copy_to(15, 3)])

    quad_devs = (sib, quad_same, quad_diag)
    start_when(d == 0, [agg_copy(at_z(step), ag_ssem.at[k]) for k, step in enumerate(TREE)])
    p_out = [[p_copy(t, at_z(step), p_ssem.at[t, k]) for k, step in enumerate(TREE)] for t in range(2)]

    for t in range(2):
        start_when(d == 0, p_out[t])
    quad_in = [start(remote(agg_mine, agg_quad.at[k + 1], q_ssem.at[k], q_rsem.at[k], quad_devs[k])) for k in range(3)]

    loads[5].wait()

    def left_product(s):
        live = s < count_ref[0, 0]
        left = jnp.dot(p_ref[rows_ref[0, 0, s]], a_buf[s], preferred_element_type=F32)
        left = jnp.where(live, left, 0.0)
        high = left.astype(BF16)
        lhl[s, 0:64] = high
        lhl[s, 64:128] = (left - high.astype(F32)).astype(BF16)

    pl.loop(0, 16)(left_product)

    for copy in quad_in:
        copy.wait_recv()
    to_smem = pltpu.make_async_copy(agg_quad, quad_s, sm_sem)
    to_smem.start()
    to_smem.wait()
    labels = [quad_s[g // 4, 0, g % 4] for g in range(16)]
    for g in range(16):
        before = jnp.int32(0)
        for o in range(g):
            before = jnp.where(labels[o] == labels[g], o + 1, before)
        rows_s[0, g] = before
    for k, step in enumerate((0,) + FAR):
        wanted = relay_ref[((z + step) % NZ) * 2 + core]
        at = jnp.int32(0)
        for g in range(16):
            at = jnp.where(labels[g] == wanted, g + 1, at)
        rows_s[1, k] = at

    @pl.when(d != 0)
    def _():
        agg_copy(at_z(1), ag_ssem.at[0]).wait_recv()

    pass_on(lambda step, k: agg_copy(at_z(step), af_ssem.at[k]))
    start(remote(agg_col.at[core], agg_col.at[core], as_ssem, as_rsem, sib))

    keys_in = []
    for k in range(1, 4):
        keys_in.append(remote(keys_x.at[0], keys_x.at[k], k_ssem.at[0, k - 1], k_rsem.at[0, k - 1], at_xy(k, 0)))
        keys_in.append(remote(keys_y.at[0], keys_y.at[k], k_ssem.at[1, k - 1], k_rsem.at[1, k - 1], at_xy(0, k)))
    for copy in keys_in:
        pending.append(copy.wait_send)

    def keys_out():
        remote(agg_col.at[1 - core], agg_col.at[1 - core], as_ssem, as_rsem, sib).wait_recv()
        to_smem = pltpu.make_async_copy(agg_col, col_s, sm_sem)
        to_smem.start()
        to_smem.wait()
        for s in range(16):
            j = cols_ref[0, 0, s]
            key = rows_ref[0, 0, s] * 32 + col_s[j // 4, 0, j % 4]
            line = jnp.full((1, 128), jnp.where(s < count_ref[0, 0], key, -1), jnp.int32)
            keys_x[0, s : s + 1] = line
            keys_y[0, s : s + 1] = line
        for copy in keys_in:
            copy.start()

    outside = (d != 0) & jnp.logical_not(in_tree)

    @pl.when(jnp.logical_not(in_tree))
    def _():
        keys_out()

    @pl.when(d != 0)
    def _():
        p_copy(0, at_z(1), p_ssem.at[0, 0]).wait_recv()

    pass_on(lambda step, k: p_copy(0, at_z(step), f_ssem.at[0, k]))
    start(remote(own_half(0), own_half(0), sib_ssem.at[0], sib_rsem.at[0], sib))

    @pl.when(in_tree)
    def _():
        p_copy(1, at_z(1), p_ssem.at[1, 0]).wait_recv()

    pass_on(lambda step, k: p_copy(1, at_z(step), f_ssem.at[1, k]))

    @pl.when(in_tree)
    def _():
        keys_out()

    def sibling_in(t):
        other = p_buf[t].at[1 - core]
        remote(other, other, sib_ssem.at[t], sib_rsem.at[t], sib).wait_recv()

    group = lax.broadcasted_iota(jnp.int32, (64, 128), 1) // 32
    small_group = lax.broadcasted_iota(jnp.int32, (32, 128), 1) // 32
    low = small_group < 2

    def product(t, s, v):
        j = cols_ref[0, 0, s]
        both = jnp.dot(lhl[s], p_buf[t][j // 4], preferred_element_type=F32)
        return pltpu.roll(both[0:64] + both[64:128], ((v + 4 - j % 4) % 4) * 32, 1)

    first_a, first_b = ([], []), ([], [])

    def products_out(t):
        @pl.loop(0, 4)
        def _(u):
            four = product(t, 4 * u, 0)
            for v in range(1, 4):
                four = jnp.where(group == v, product(t, 4 * u + v, v), four)
            g_a[t, 0, u] = four[0:32]
            g_b[t, 0, u] = four[32:64]

        for k in range(1, 4):
            first_a[t].append(start(remote(g_a.at[t, 0], g_a.at[t, k], x_ssem.at[t, 0, k - 1], x_rsem.at[t, 0, k - 1], at_xy(k, 0))))
            first_b[t].append(start(remote(g_b.at[t, 0], g_b.at[t, k], x_ssem.at[t, 1, k - 1], x_rsem.at[t, 1, k - 1], at_xy(0, k))))

    sibling_in(0)
    products_out(0)

    @pl.when(outside)
    def _():
        p_copy(1, at_z(1), p_ssem.at[1, 0]).wait_recv()

    start(remote(own_half(1), own_half(1), sib_ssem.at[1], sib_rsem.at[1], sib))

    for copy in keys_in:
        copy.wait_recv()
    lane_i = lax.broadcasted_iota(jnp.int32, (64, 128), 1)
    slot_i = lax.broadcasted_iota(jnp.int32, (64, 128), 0)
    table[...] = jnp.zeros((8, 128), jnp.int32)
    for h, keys in enumerate((keys_x, keys_y)):
        down = keys[...].reshape(64, 128)
        across = jnp.sum(jnp.where(slot_i == lane_i, down, 0), axis=0, keepdims=True)
        before = jnp.where((down == across) & (slot_i < lane_i), slot_i + 1, 0)
        table[2 * h : 2 * h + 1] = jnp.max(before, axis=0, keepdims=True)
        table[2 * h + 1 : 2 * h + 2] = jnp.max(jnp.where(down == lane_i, slot_i + 1, 0), axis=0, keepdims=True)
    to_smem = pltpu.make_async_copy(table, table_s, sm_sem)
    to_smem.start()

    sibling_in(1)
    products_out(1)
    to_smem.wait()

    run_a[0] = jnp.zeros((32, 128), F32)
    run_b[0] = jnp.zeros((32, 128), F32)
    second_a, second_b = ([], []), ([], [])

    def join(parts):
        left = jnp.where(small_group == 0, parts[0], parts[1])
        return jnp.where(low, left, jnp.where(small_group == 2, parts[2], parts[3]))

    def blocks(run, h, first_key):
        return join([run[table_s[2 * h + 1, first_key + o]] for o in (0, 1, 32, 33)])

    def sums_out(t):
        for k in range(4):
            if k:
                first_a[t][k - 1].wait_recv()
                first_b[t][k - 1].wait_recv()

            @pl.loop(0, 4)
            def _(u):
                for h, (got, run) in enumerate(((g_a, run_a), (g_b, run_b))):
                    turned = [got[t, k, u]]
                    for o in range(1, 4):
                        turned.append(pltpu.roll(turned[0], 32 * o, 1))
                    for v in range(4):
                        s = k * 16 + 4 * u + v
                        parts = [turned[(g + 4 - v) % 4] for g in range(4)]
                        run[s + 1] = join(parts) + run[table_s[2 * h, s]]

        for k in (1, 2, 3, 0):
            there = ((y + k) % NY) * NX + x
            for n in range(2):
                e_a[t, k, n] = blocks(run_a, 0, n * 64 + there * 2)
            if k:
                second_a[t].append(start(remote(e_a.at[t, k], r2_a.at[t, k - 1], x2_ssem.at[t, 0, k - 1], x2_rsem.at[t, 0, k - 1], at_xy(0, k))))
            there = y * NX + (x + k) % NX
            for n in range(2):
                e_b[t, k, n] = blocks(run_b, 1, n * 64 + there * 2)
            if k:
                second_b[t].append(start(remote(e_b.at[t, k], r2_b.at[t, k - 1], x2_ssem.at[t, 1, k - 1], x2_rsem.at[t, 1, k - 1], at_xy(k, 0))))

    sums_out(0)
    sums_out(1)

    to_pair, to_sib, on_sib = [], [], []
    for h in range(2):
        for copy in second_a[h] + second_b[h]:
            copy.wait_recv()
        for n in range(2):
            top = (e_a[h, 0, n] + r2_a[h, 0, n]) + (r2_a[h, 1, n] + r2_a[h, 2, n])
            bottom = (e_b[h, 0, n] + r2_b[h, 0, n]) + (r2_b[h, 1, n] + r2_b[h, 2, n])
            quad[0, h, 2 * n] = jnp.where(low, top, pltpu.roll(bottom, 64, 1))
            quad[0, h, 2 * n + 1] = jnp.where(low, pltpu.roll(top, 64, 1), bottom)
        to_pair.append(start(remote(quad.at[0, h], quad.at[2, h], z_ssem.at[h, 1], z_rsem.at[h, 1], quad_same)))
        to_sib.append(start(remote(quad.at[0, h], quad.at[1, h], z_ssem.at[h, 0], z_rsem.at[h, 0], sib)))
        on_sib.append(remote(quad.at[2, h], quad.at[3, h], z_ssem.at[h, 2], z_rsem.at[h, 2], sib))

    def chain(h, group):
        for g in range(group * 4, group * 4 + 4):
            run_z[h, g + 1] = quad[group, h, g % 4] + run_z[h, rows_s[0, g]]

    far, far_scale = ([], []), ([], [])
    diagonal = lax.broadcasted_iota(jnp.int32, (32, 128), 0) == lax.broadcasted_iota(jnp.int32, (32, 128), 1)
    for h in range(2):
        run_z[h, 0] = jnp.zeros((32, 128), F32)
        chain(h, 0)
        to_sib[h].wait_recv()
        chain(h, 1)
        to_pair[h].wait_recv()
        start(on_sib[h])
        chain(h, 2)
        on_sib[h].wait_recv()
        chain(h, 3)
        own[h] = run_z[h, rows_s[1, 0]]
        for k, step in enumerate(FAR):
            block = run_z[h, rows_s[1, k + 1]]
            largest = jnp.maximum(jnp.max(jnp.abs(block), axis=1, keepdims=True), 1e-30)
            ob[h, k] = jnp.round(block * (STEPS / largest)).astype(jnp.int32).astype(jnp.int16)
            scale[h, k] = jnp.sum(jnp.where(diagonal, largest, 0.0), axis=0, keepdims=True)
            far[h].append(start(remote(ob.at[h, k], rz.at[h, k], w_ssem.at[h, k], w_rsem.at[h, k], at_z(step))))
            far_scale[h].append(start(remote(scale.at[h, k], scale_in.at[h, k], v_ssem.at[h, k], v_rsem.at[h, k], at_z(step))))

    spread = ([], [])
    for h in range(2):
        total = own[h]
        for k in range(len(FAR)):
            far_scale[h][k].wait_recv()
            largest = jnp.sum(jnp.where(diagonal, scale_in[h, k], 0.0), axis=1, keepdims=True)
            far[h][k].wait_recv()
            total = total + rz[h, k].astype(jnp.int32).astype(F32) * (largest / STEPS)
        tile[h] = total
        for k, (dx, dy) in enumerate(plane):
            spread[h].append(start(remote(tile.at[h], gat.at[h, k], o_ssem.at[h, k], o_rsem.at[h, k], at_xy(dx, dy))))

    def place(source, first, second):
        there = pl.ds(pl.multiple_of(source * 128, 128), 128)
        out_ref[0, 0:32, there] = jnp.where(
            low,
            jnp.where(small_group == 0, first, pltpu.roll(second, 32, 1)),
            jnp.where(small_group == 2, pltpu.roll(first, 32, 1), pltpu.roll(second, 64, 1)),
        )
        out_ref[0, 32:64, there] = jnp.where(
            low,
            jnp.where(small_group == 0, pltpu.roll(first, 64, 1), pltpu.roll(second, 96, 1)),
            jnp.where(small_group == 2, pltpu.roll(first, 96, 1), second),
        )

    place(col, tile[0], tile[1])
    for copy in spread[0]:
        copy.wait_recv()
    for k, (dx, dy) in enumerate(plane):
        spread[1][k].wait_recv()
        source = ((y + NY - dy) % NY) * NX + (x + NX - dx) % NX
        place(source, gat[0, k], gat[1, k])
    finish()


def on_device(a_blocks, slot_row, slot_col, slot_count, p_blocks, aggregate, relayout):
    hbm = pl.BlockSpec(memory_space=pltpu.HBM)
    vmem = pl.BlockSpec(memory_space=pltpu.VMEM)
    dma = pltpu.SemaphoreType.DMA
    return pl.pallas_call(
        kernel,
        out_shape=pltpu.VMEM((1, 64, 2048), F32),
        in_specs=[hbm, hbm, hbm, hbm, vmem, hbm, hbm],
        out_specs=vmem,
        scratch_shapes=[
            pltpu.VMEM((16, 320, 320), BF16),
            pltpu.VMEM((16, 128, 320), BF16),
            pltpu.VMEM((2, 320, 128), BF16),
            pltpu.VMEM((2, 320, 128), BF16),
            pltpu.SMEM((1, 1, 16), jnp.int32),
            pltpu.SMEM((1, 1, 16), jnp.int32),
            pltpu.SMEM((1, 1), jnp.int32),
            pltpu.SMEM((4,), jnp.int32),
            pltpu.SMEM((32,), jnp.int32),
            pltpu.VMEM((8, 128), jnp.int32),
            pltpu.VMEM((2, 8, 128), jnp.int32),
            pltpu.VMEM((4, 8, 128), jnp.int32),
            pltpu.VMEM((4, 16, 128), jnp.int32),
            pltpu.VMEM((4, 16, 128), jnp.int32),
            pltpu.VMEM((8, 128), jnp.int32),
            pltpu.SMEM((2, 8, 128), jnp.int32),
            pltpu.SMEM((4, 8, 128), jnp.int32),
            pltpu.SMEM((8, 128), jnp.int32),
            pltpu.SMEM((2, 16), jnp.int32),
            pltpu.VMEM((2, 4, 4, 32, 128), F32),
            pltpu.VMEM((2, 4, 4, 32, 128), F32),
            pltpu.VMEM((65, 32, 128), F32),
            pltpu.VMEM((65, 32, 128), F32),
            pltpu.VMEM((2, 4, 2, 32, 128), F32),
            pltpu.VMEM((2, 4, 2, 32, 128), F32),
            pltpu.VMEM((2, 3, 2, 32, 128), F32),
            pltpu.VMEM((2, 3, 2, 32, 128), F32),
            pltpu.VMEM((4, 2, 4, 32, 128), F32),
            pltpu.VMEM((2, 17, 32, 128), F32),
            pltpu.VMEM((2, 32, 128), F32),
            pltpu.VMEM((2, 7, 32, 128), jnp.int16),
            pltpu.VMEM((2, 7, 32, 128), jnp.int16),
            pltpu.VMEM((2, 7, 1, 128), F32),
            pltpu.VMEM((2, 7, 1, 128), F32),
            pltpu.VMEM((2, 32, 128), F32),
            pltpu.VMEM((2, 15, 32, 128), F32),
            dma((6,)), dma,
            dma((2, 4)), dma((2,)), dma((2, 4)), dma((2,)), dma((2,)),
            dma((4,)), dma, dma((4,)), dma, dma,
            dma((3,)), dma((3,)), dma((2, 3)), dma((2, 3)),
            dma((2, 2, 3)), dma((2, 2, 3)), dma((2, 2, 3)), dma((2, 2, 3)),
            dma((2, 3)), dma((2, 3)), dma((2, 7)), dma((2, 7)), dma((2, 7)), dma((2, 7)), dma((2, 15)), dma((2, 15)),
        ],
        compiler_params=pltpu.CompilerParams(
            collective_id=0, has_side_effects=True, vmem_limit_bytes=60 << 20
        ),
        name="coarse_operator",
    )(a_blocks, slot_row, slot_col, slot_count, jnp.swapaxes(p_blocks, 1, 2), aggregate, relayout)


def solution(mesh):
    return jax.shard_map(
        on_device,
        mesh=mesh,
        in_specs=(
            P("row", "col", None, None, None),
            P("row", "col", None),
            P("row", "col", None),
            P("row", "col"),
            P("row", None, None),
            P("row"),
            P(),
        ),
        out_specs=P("row", None, None),
        check_vma=False,
    )
```
